32 devices in a mesh: mode: 2 (over x), ax: 8 (over z, y), rad: 2 (over core).
Axes of the slice: x: 2, y: 2, z: 4, core: 2. Of those that a mesh axis runs over, the one named last changes fastest.
Arguments:
- adjoint: float32 [5, 256, 32, 256], P(None, 'mode', 'ax', 'rad'), may hold values from -6 to 6
- state: float32 [5, 256, 32, 256], P(None, 'mode', 'ax', 'rad'), may hold values from -6 to 6
- wake: float32 [256, 32, 256], P('mode', 'ax', 'rad'), may hold values from 0.2 to 1.5
- jac_axial: float32 [5, 5], replicated, may hold values from -2.5 to 2.5
- jac_radial: float32 [5, 5], replicated, may hold values from -2.5 to 2.5
- jac_swirl: float32 [5, 5], replicated, may hold values from -2.5 to 2.5
- wake_coupling: float32 [5, 5], replicated, may hold values from -2.5 to 2.5
Outputs:
- adjoint_in: float32 [5, 256, 32, 256], P(None, 'mode', 'ax', 'rad')
- wake_grad: float32 [256, 32, 256], P('mode', 'ax', 'rad')
The draws below stay inside these ranges and needn't reach their ends.
All inputs are finite; a program needn't handle non-finite values.
Results may differ from the reference program's by a relative error of at most 0.000098.
Values sent between devices are 32-bit elements; how exact they have to be, the bound alone decides.
No kernel may reach another device: no remote copies, remote signals or barrier semaphores. Data moves between devices by JAX's collectives and lax.ppermute only.
A program may use at most 64 MiB of HBM per device.

```python
import math
import jax
import jax.numpy as jnp
from jax import lax

F = 5
M = 256
CXD = 4
NX = 32
NR = 256


def levels(rng, dims, shards, smallest, largest):
    level, own = 1.0, jax.random.fold_in(rng, 6)
    for position, shards_of in shards:
        steps = jnp.exp(jax.random.uniform(jax.random.fold_in(own, position), (shards_of,), jnp.float32, smallest / len(shards), largest / len(shards)))
        level = level * jnp.repeat(steps, dims[position] // shards_of).reshape([-1 if axis == position else 1 for axis in range(len(dims))])
    return level


def normal_values(stream_key, extent, width, bound, pieces=(), kind=jnp.bfloat16):
    entries = width * jax.random.normal(stream_key, extent, jnp.float32)
    if pieces:
        entries = entries * levels(stream_key, extent, pieces, -0.22, 0.18)
    return jnp.clip(entries, -bound, bound).astype(kind)


def setup_inputs(seed: int = 0) -> dict:
    keys = jax.random.split(jax.random.key(seed), 8)
    adjoint = normal_values(keys[0], (F, M, NX, NR), 1.0, 6.0, ((1, 2), (2, 8), (3, 2)), jnp.float32)
    state = normal_values(keys[1], (F, M, NX, NR), 1.0, 6.0, ((1, 2), (2, 8), (3, 2)), jnp.float32)
    wake = jnp.clip(0.2 + 1.3 * jax.random.uniform(keys[2], (M, NX, NR), jnp.float32) ** levels(keys[2], (M, NX, NR), ((0, 2), (1, 8), (2, 2)), -0.2, 0.2), 0.2, 1.5)
    jac_axial = normal_values(keys[3], (F, F), F ** -0.5, 2.5, (), jnp.float32)
    jac_radial = normal_values(keys[4], (F, F), F ** -0.5, 2.5, (), jnp.float32)
    jac_swirl = normal_values(keys[5], (F, F), F ** -0.5, 2.5, (), jnp.float32)
    wake_coupling = normal_values(keys[6], (F, F), F ** -0.5, 2.5, (), jnp.float32)
    return dict(adjoint=adjoint, state=state, wake=wake, jac_axial=jac_axial, jac_radial=jac_radial, jac_swirl=jac_swirl, wake_coupling=wake_coupling)


exact_prec = lax.Precision.HIGHEST

def fourier_basis(mode_count):
    angle_idx = jnp.arange(mode_count, dtype=jnp.int32)[:, None]
    coef_idx = jnp.arange(mode_count, dtype=jnp.int32)[None, :]
    orders = coef_idx // 2
    phases = (orders * angle_idx % mode_count).astype(jnp.float32) * jnp.float32(2.0 * math.pi / mode_count)
    scale_two = jnp.float32(math.sqrt(2.0 / mode_count))
    scale_one = jnp.float32(1.0 / math.sqrt(mode_count))
    table = jnp.where(coef_idx % 2 == 0, scale_two * jnp.cos(phases), scale_two * jnp.sin(phases))
    table = jnp.where(coef_idx == 0, scale_one, table)
    signs = jnp.where(angle_idx % 2 == 0, scale_one, -scale_one)
    table = jnp.where(coef_idx == 1, signs, table)
    return table

def rotate(field, first_order, mode_count):
    fields, modes_here, cells_ax, cells_rad = field.shape
    paired = field.reshape(fields, modes_here // 2, 2, cells_ax, cells_rad)
    orders = (first_order + jnp.arange(modes_here // 2, dtype=jnp.int32)).astype(jnp.float32) / jnp.float32(mode_count // 2)
    orders = orders[None, :, None, None]
    turned = jnp.stack([orders * paired[:, :, 1], -orders * paired[:, :, 0]], axis=2)
    return turned.reshape(fields, modes_here, cells_ax, cells_rad)

def reference(adjoint, state, wake, jac_axial, jac_radial, jac_swirl, wake_coupling):
    padded = jnp.pad(adjoint, ((0, 0), (0, 0), (1, 1), (1, 1)))
    axial_diff = 0.5 * (padded[:, :, 2:, 1:-1] - padded[:, :, :-2, 1:-1])
    radial_diff = 0.5 * (padded[:, :, 1:-1, 2:] - padded[:, :, 1:-1, :-2])
    radius = 0.5 + (jnp.arange(NR, dtype=jnp.int32).astype(jnp.float32) + 0.5) / jnp.float32(2.0 * NR)
    swirl_rate = 0.25 / radius
    turned = rotate(adjoint, 0, M) * swirl_rate
    transport = jnp.einsum('ef,ekxr->fkxr', jac_axial, axial_diff, precision=exact_prec)
    transport = transport + jnp.einsum('ef,ekxr->fkxr', jac_radial, radial_diff, precision=exact_prec)
    transport = transport + jnp.einsum('ef,ekxr->fkxr', jac_swirl, turned, precision=exact_prec)
    coupled = jnp.einsum('fe,ekxr->fkxr', wake_coupling, state, precision=exact_prec)
    basis_table = fourier_basis(M)

    def block_part(offset):
        adj_part = lax.dynamic_slice_in_dim(adjoint, offset, CXD, 2)
        cpl_part = lax.dynamic_slice_in_dim(coupled, offset, CXD, 2)
        wake_part = lax.dynamic_slice_in_dim(wake, offset, CXD, 1)
        adj_angle = jnp.einsum('tk,fkxr->ftxr', basis_table, adj_part, precision=exact_prec)
        cpl_angle = jnp.einsum('tk,fkxr->ftxr', basis_table, cpl_part, precision=exact_prec)
        returned = jnp.einsum('tk,ftxr->fkxr', basis_table, wake_part[None] * adj_angle, precision=exact_prec)
        grad_part = -lax.optimization_barrier(jnp.sum(adj_angle * cpl_angle, axis=0))
        return (returned, grad_part)
    offsets = jnp.arange(NX // CXD, dtype=jnp.int32) * CXD
    returned_all, grad_all = lax.map(block_part, offsets)
    returned = jnp.moveaxis(returned_all, 0, 2).reshape(F, M, NX, NR)
    wake_grad = jnp.moveaxis(grad_all, 0, 1).reshape(M, NX, NR)
    adjoint_in = adjoint + transport - jnp.einsum('ef,ekxr->fkxr', wake_coupling, returned, precision=exact_prec)
    return (adjoint_in, wake_grad)
```

```python
import functools
import math

import jax
import jax.numpy as jnp
import ml_dtypes
import numpy as np
from jax import lax
from jax.experimental import pallas as pl
from jax.experimental.pallas import tpu as pltpu
from jax.sharding import PartitionSpec as P

VMEM_LIMIT = 32 * 1024 * 1024


def fourier_basis(count):
    angle = np.arange(count)[:, None]
    coef = np.arange(count)[None, :]
    phase = ((coef // 2) * angle % count) * (2.0 * math.pi / count)
    table = math.sqrt(2.0 / count) * np.where(coef % 2 == 0, np.cos(phase), np.sin(phase))
    table = np.where(coef == 0, 1.0 / math.sqrt(count), table)
    table = np.where(coef == 1, np.where(angle % 2 == 0, 1.0, -1.0) / math.sqrt(count), table)
    return table.astype(np.float32)


def three_terms(table):
    high = table.astype(ml_dtypes.bfloat16)
    low = (table - high.astype(np.float32)).astype(ml_dtypes.bfloat16)
    return np.concatenate([high, low, high], axis=-1)


def tables(groups, modes_here):
    count = groups * modes_here
    basis = fourier_basis(count)
    own, other, back = [], [], []
    for m in range(groups):
        rolled = np.roll(np.roll(basis, -m * modes_here, axis=0), -m * modes_here, axis=1)
        blocks = [rolled[:, s * modes_here : (s + 1) * modes_here] for s in range(groups)]
        own.append(three_terms(blocks[0]))
        other.append(np.stack([three_terms(block) for block in blocks[1:]]))
        back.append(three_terms(np.ascontiguousarray(blocks[0].T)))
    return np.stack(own), np.stack(other), np.stack(back)


def split(value):
    high = value.astype(jnp.bfloat16)
    low = (value - high.astype(jnp.float32)).astype(jnp.bfloat16)
    return high, low


def put_split(terms, row, rows, total, cols, value):
    high, low = split(value)
    terms[pl.ds(row, rows), cols] = high
    terms[pl.ds(total + row, rows), cols] = high
    terms[pl.ds(2 * total + row, rows), cols] = low


def own_kernel(dims, where, adj, state, coupling, table, a_out, c_out, terms_a, terms_c):
    fields, modes, cells_ax, width, cols_of = dims
    for j in range(width):
        x = pl.program_id(0) * width + j
        rows = pl.ds(x, modes, stride=cells_ax)
        for f in range(fields):
            put_split(terms_a, 0, modes, modes, cols_of(j, f), adj[f, rows, :])
    a_out[0] = jnp.dot(table[0], terms_a[...], preferred_element_type=jnp.float32)
    for j in range(width):
        x = pl.program_id(0) * width + j
        rows = pl.ds(x, modes, stride=cells_ax)
        for f in range(fields):
            mixed = coupling[f, 0] * state[0, rows, :]
            for e in range(1, fields):
                mixed = mixed + coupling[f, e] * state[e, rows, :]
            put_split(terms_c, 0, modes, modes, cols_of(j, f), mixed)
    c_out[0] = jnp.dot(table[0], terms_c[...], preferred_element_type=jnp.float32)


def join_kernel(dims, groups, where, *refs):
    fields, modes, cells_ax, width, cols_of = dims
    recv = refs[: groups - 1]
    a_own, c_own, table, a_out = refs[groups - 1 : groups + 3]
    h_out = refs[groups + 3 : 2 * groups + 3]
    terms = refs[2 * groups + 3]
    total = a_own[0]
    for s in range(groups - 1):
        for j in range(width):
            x = pl.program_id(0) * width + j
            rows = pl.ds(x, modes, stride=cells_ax)
            for f in range(fields):
                put_split(terms, 0, modes, modes, cols_of(j, f), recv[s][f, rows, :])
        total = total + jnp.dot(table[0, s], terms[...], preferred_element_type=jnp.float32)
    a_out[0] = total
    for j in range(width):
        x = pl.program_id(0) * width + j
        rows = pl.ds(x, modes, stride=cells_ax)
        for s in range(groups):
            here = pl.ds(s * modes, modes)
            part = a_out[0, here, cols_of(j, 0)] * c_own[0, here, cols_of(j, 0)]
            for f in range(1, fields):
                part = part + a_out[0, here, cols_of(j, f)] * c_own[0, here, cols_of(j, f)]
            h_out[s][rows, :] = part


def back_kernel(dims, groups, where, *refs):
    fields, modes, cells_ax, width, cols_of = dims
    wakes = refs[:groups]
    angle, base, coupling, table, out, terms = refs[groups:]
    count = groups * modes
    for j in range(width):
        x = pl.program_id(0) * width + j
        rows = pl.ds(x, modes, stride=cells_ax)
        for s in range(groups):
            wake = wakes[s][rows, :]
            for f in range(fields):
                scaled = wake * angle[0, pl.ds(s * modes, modes), cols_of(j, f)]
                put_split(terms, s * modes, modes, count, cols_of(j, f), scaled)
    returned = jnp.dot(table[0], terms[...], preferred_element_type=jnp.float32)
    for j in range(width):
        x = pl.program_id(0) * width + j
        rows = pl.ds(x, modes, stride=cells_ax)
        for f in range(fields):
            value = base[f, rows, :]
            for e in range(fields):
                value = value - coupling[e, f] * returned[:, cols_of(j, e)]
            out[f, rows, :] = value


def base_kernel(
    fields, modes, cells_ax, chunk, mode_total, rad_total, rad_size,
    where, adj, below, above, inner, outer, jac_axial, jac_radial, jac_swirl, out,
):
    lanes = adj.shape[2]
    half = modes // 2
    rad = where[1]
    lane = lax.broadcasted_iota(jnp.int32, (chunk, lanes), 1)
    row = lax.broadcasted_iota(jnp.int32, (chunk, lanes), 0)
    radius = 0.5 + ((rad * lanes + lane).astype(jnp.float32) + 0.5) / jnp.float32(2.0 * rad_total)
    swirl = 0.25 / radius
    has_inner = jnp.where((lane == 0) & (rad == 0), 0.0, 0.5)
    has_outer = jnp.where((lane == lanes - 1) & (rad == rad_size - 1), 0.0, 0.5)

    def step(i, carry):
        order = (where[0] * half + i * chunk + row).astype(jnp.float32) / jnp.float32(mode_total // 2)
        rate = swirl * order
        for p in range(2):
            halo = pl.ds(2 * i * chunk + p, chunk, stride=2)
            for x in range(cells_ax):
                def at(e, parity, cell):
                    start = (2 * i * chunk + parity) * cells_ax + cell
                    return adj[e, pl.ds(start, chunk, stride=2 * cells_ax), :]

                here = pl.ds((2 * i * chunk + p) * cells_ax + x, chunk, stride=2 * cells_ax)
                total = [None] * fields
                for e in range(fields):
                    centre = at(e, p, x)
                    low = below[e, halo, :] if x == 0 else at(e, p, x - 1)
                    high = above[e, halo, :] if x == cells_ax - 1 else at(e, p, x + 1)
                    axial = 0.5 * (high - low)
                    from_inner = jnp.where(lane == lanes - 1, inner[e, here, :], centre)
                    from_outer = jnp.where(lane == 0, outer[e, here, :], centre)
                    radial = has_outer * pltpu.roll(from_outer, lanes - 1, 1) - has_inner * pltpu.roll(
                        from_inner, 1, 1
                    )
                    turned = (rate if p == 0 else -rate) * at(e, 1 - p, x)
                    for f in range(fields):
                        term = (
                            jac_axial[e, f] * axial
                            + jac_radial[e, f] * radial
                            + jac_swirl[e, f] * turned
                        )
                        if f == e:
                            term = term + centre
                        total[f] = term if e == 0 else total[f] + term
                for f in range(fields):
                    out[f, here, :] = total[f]
        return carry

    lax.fori_loop(0, half // chunk, step, 0)


def whole(shape):
    return pl.BlockSpec(shape, lambda i, where: (0,) * len(shape))


def stepped(shape):
    return pl.BlockSpec((1, *shape[1:]), lambda i, where: (i,) + (0,) * (len(shape) - 1))


def chosen(shape):
    return pl.BlockSpec((1, *shape[1:]), lambda i, where: (where[0],) + (0,) * (len(shape) - 1))


SMEM = pl.BlockSpec(memory_space=pltpu.SMEM)


def call(kernel, steps, where, args, in_specs, outs, out_specs, scratch, flops):
    moved = sum(a.size * a.dtype.itemsize for a in args) + sum(o.size * o.dtype.itemsize for o in outs)
    return pl.pallas_call(
        kernel,
        grid_spec=pltpu.PrefetchScalarGridSpec(
            num_scalar_prefetch=1,
            grid=(steps,),
            in_specs=in_specs,
            out_specs=out_specs,
            scratch_shapes=scratch,
        ),
        out_shape=outs,
        compiler_params=pltpu.CompilerParams(vmem_limit_bytes=VMEM_LIMIT),
        cost_estimate=pl.CostEstimate(flops=flops, bytes_accessed=moved, transcendentals=0),
    )(where, *args)


def body(adjoint, state, wake, jac_axial, jac_radial, jac_swirl, wake_coupling):
    fields, modes, cells_ax, lanes = adjoint.shape
    groups = lax.axis_size("mode")
    count = groups * modes
    rad_size = lax.axis_size("rad")
    ax_size = lax.axis_size("ax")
    width = 2 if cells_ax % 2 == 0 else 1
    steps = cells_ax // width
    rows = modes * cells_ax
    cols = width * fields * lanes
    f32 = jnp.float32

    def cols_of(j, f):
        return pl.ds((j * fields + f) * lanes, lanes)

    dims = (fields, modes, cells_ax, width, cols_of)
    own_table, other_table, back_table = tables(groups, modes)
    where = jnp.stack([lax.axis_index("mode"), lax.axis_index("rad")]).astype(jnp.int32)

    adj = adjoint.reshape(fields, rows, lanes)
    st = state.reshape(fields, rows, lanes)
    wk = wake.reshape(rows, lanes)

    def fetch(value, s):
        return lax.ppermute(value, "mode", [((i + s) % groups, i) for i in range(groups)])

    def deliver(value, s):
        return lax.ppermute(value, "mode", [(i, (i + s) % groups) for i in range(groups)])

    adj_recv = [fetch(adj, s) for s in range(1, groups)]

    up = [(i, i + 1) for i in range(ax_size - 1)]
    down = [(i + 1, i) for i in range(ax_size - 1)]
    below = lax.ppermute(adjoint[:, :, cells_ax - 1, :], "ax", up)
    above = lax.ppermute(adjoint[:, :, 0, :], "ax", down)
    if rad_size == 2:
        inner = outer = lax.ppermute(adj, "rad", [(0, 1), (1, 0)])
    else:
        inner = lax.ppermute(adj, "rad", [(i, i + 1) for i in range(rad_size - 1)])
        outer = lax.ppermute(adj, "rad", [(i + 1, i) for i in range(rad_size - 1)])
    wake_recv = [fetch(wk, s) for s in range(1, groups)]

    field_shape = (fields, rows, lanes)
    angle_shape = (steps, count, cols)
    angle = jax.ShapeDtypeStruct(angle_shape, f32)
    field = jax.ShapeDtypeStruct(field_shape, f32)
    plane = jax.ShapeDtypeStruct((rows, lanes), f32)
    own_flops = 2 * 2 * 3 * count * modes * steps * cols

    a_own, c_own = call(
        functools.partial(own_kernel, dims), steps, where,
        (adj, st, wake_coupling, own_table),
        [whole(field_shape), whole(field_shape), SMEM, chosen(own_table.shape)],
        [angle, angle],
        [stepped(angle_shape), stepped(angle_shape)],
        [pltpu.VMEM((3 * modes, cols), jnp.bfloat16)] * 2,
        own_flops,
    )

    chunk = 16 if modes % 32 == 0 else 8
    base = call(
        functools.partial(
            base_kernel, fields, modes, cells_ax, chunk, count, lanes * rad_size, rad_size
        ),
        1, where,
        (adj, below, above, inner, outer, jac_axial, jac_radial, jac_swirl),
        [whole(field_shape), whole(below.shape), whole(above.shape)]
        + [whole(field_shape)] * 2 + [SMEM] * 3,
        [field], [whole(field_shape)], [],
        32 * fields * fields * rows * lanes,
    )[0]

    joined = call(
        functools.partial(join_kernel, dims, groups), steps, where,
        (*adj_recv, a_own, c_own, other_table),
        [whole(field_shape)] * (groups - 1)
        + [stepped(angle_shape), stepped(angle_shape), chosen(other_table.shape)],
        [angle] + [plane] * groups,
        [stepped(angle_shape)] + [whole((rows, lanes))] * groups,
        [pltpu.VMEM((3 * modes, cols), jnp.bfloat16)],
        (groups - 1) * own_flops // 2,
    )
    a_all, parts = joined[0], joined[1:]
    part_recv = [deliver(parts[s], s) for s in range(1, groups)]

    adjoint_in = call(
        functools.partial(back_kernel, dims, groups), steps, where,
        (wk, *wake_recv, a_all, base, wake_coupling, back_table),
        [whole((rows, lanes))] * groups
        + [stepped(angle_shape), whole(field_shape), SMEM, chosen(back_table.shape)],
        [field], [whole(field_shape)],
        [pltpu.VMEM((3 * count, cols), jnp.bfloat16)],
        own_flops // 2,
    )[0]

    total = parts[0]
    for part in part_recv:
        total = total + part
    return (
        adjoint_in.reshape(adjoint.shape),
        (-total).reshape(wake.shape),
    )


def solution(mesh):
    return jax.shard_map(
        body,
        mesh=mesh,
        in_specs=(
            P(None, "mode", "ax", "rad"),
            P(None, "mode", "ax", "rad"),
            P("mode", "ax", "rad"),
            P(),
            P(),
            P(),
            P(),
        ),
        out_specs=(P(None, "mode", "ax", "rad"), P("mode", "ax", "rad")),
        check_vma=False,
    )
```

```python
import functools
import math

import jax
import jax.numpy as jnp
import ml_dtypes
import numpy as np
from jax import lax
from jax.experimental import pallas as pl
from jax.experimental.pallas import tpu as pltpu
from jax.sharding import PartitionSpec as P

VMEM_LIMIT = 32 * 1024 * 1024


def fourier_basis(count):
    angle = np.arange(count)[:, None]
    coef = np.arange(count)[None, :]
    phase = ((coef // 2) * angle % count) * (2.0 * math.pi / count)
    table = math.sqrt(2.0 / count) * np.where(coef % 2 == 0, np.cos(phase), np.sin(phase))
    table = np.where(coef == 0, 1.0 / math.sqrt(count), table)
    table = np.where(coef == 1, np.where(angle % 2 == 0, 1.0, -1.0) / math.sqrt(count), table)
    return table.astype(np.float32)


def three_terms(table):
    high = table.astype(ml_dtypes.bfloat16)
    low = (table - high.astype(np.float32)).astype(ml_dtypes.bfloat16)
    return np.concatenate([high, low, high], axis=-1)


def tables(groups, modes_here):
    count = groups * modes_here
    basis = fourier_basis(count)
    own, other, back = [], [], []
    for m in range(groups):
        rolled = np.roll(np.roll(basis, -m * modes_here, axis=0), -m * modes_here, axis=1)
        blocks = [rolled[:, s * modes_here : (s + 1) * modes_here] for s in range(groups)]
        own.append(three_terms(blocks[0]))
        other.append(np.stack([three_terms(block) for block in blocks[1:]]))
        back.append(three_terms(np.ascontiguousarray(blocks[0].T)))
    return np.stack(own), np.stack(other), np.stack(back)


def split(value):
    high = value.astype(jnp.bfloat16)
    low = (value - high.astype(jnp.float32)).astype(jnp.bfloat16)
    return high, low


def put_split(terms, row, rows, total, cols, value):
    high, low = split(value)
    terms[pl.ds(row, rows), cols] = high
    terms[pl.ds(total + row, rows), cols] = high
    terms[pl.ds(2 * total + row, rows), cols] = low


def own_kernel(dims, where, adj, state, coupling, table, a_out, c_out, terms_a, terms_c):
    fields, modes, cells_ax, width, cols_of = dims
    for j in range(width):
        x = pl.program_id(0) * width + j
        rows = pl.ds(x, modes, stride=cells_ax)
        for f in range(fields):
            put_split(terms_a, 0, modes, modes, cols_of(j, f), adj[f, rows, :])
    a_out[0] = jnp.dot(table[0], terms_a[...], preferred_element_type=jnp.float32)
    for j in range(width):
        x = pl.program_id(0) * width + j
        rows = pl.ds(x, modes, stride=cells_ax)
        for f in range(fields):
            mixed = coupling[f, 0] * state[0, rows, :]
            for e in range(1, fields):
                mixed = mixed + coupling[f, e] * state[e, rows, :]
            put_split(terms_c, 0, modes, modes, cols_of(j, f), mixed)
    c_out[0] = jnp.dot(table[0], terms_c[...], preferred_element_type=jnp.float32)


def join_kernel(dims, groups, where, *refs):
    fields, modes, cells_ax, width, cols_of = dims
    recv = refs[: groups - 1]
    a_own, c_own, table, _, a_out = refs[groups - 1 : groups + 4]
    h_out = refs[groups + 4 : 2 * groups + 4]
    terms = refs[2 * groups + 4]
    total = a_own[0]
    for s in range(groups - 1):
        for j in range(width):
            x = pl.program_id(0) * width + j
            rows = pl.ds(x, modes, stride=cells_ax)
            for f in range(fields):
                put_split(terms, 0, modes, modes, cols_of(j, f), recv[s][f, rows, :])
        total = total + jnp.dot(table[0, s], terms[...], preferred_element_type=jnp.float32)
    a_out[0] = total
    for j in range(width):
        x = pl.program_id(0) * width + j
        rows = pl.ds(x, modes, stride=cells_ax)
        for s in range(groups):
            here = pl.ds(s * modes, modes)
            part = a_out[0, here, cols_of(j, 0)] * c_own[0, here, cols_of(j, 0)]
            for f in range(1, fields):
                part = part + a_out[0, here, cols_of(j, f)] * c_own[0, here, cols_of(j, f)]
            h_out[s][rows, :] = part


def back_kernel(dims, groups, where, *refs):
    fields, modes, cells_ax, width, cols_of = dims
    wakes = refs[:groups]
    angle, base, coupling, table, out, terms = refs[groups:]
    count = groups * modes
    for j in range(width):
        x = pl.program_id(0) * width + j
        rows = pl.ds(x, modes, stride=cells_ax)
        for s in range(groups):
            wake = wakes[s][rows, :]
            for f in range(fields):
                scaled = wake * angle[0, pl.ds(s * modes, modes), cols_of(j, f)]
                put_split(terms, s * modes, modes, count, cols_of(j, f), scaled)
    returned = jnp.dot(table[0], terms[...], preferred_element_type=jnp.float32)
    for j in range(width):
        x = pl.program_id(0) * width + j
        rows = pl.ds(x, modes, stride=cells_ax)
        for f in range(fields):
            value = base[f, rows, :]
            for e in range(fields):
                value = value - coupling[e, f] * returned[:, cols_of(j, e)]
            out[f, rows, :] = value


def base_kernel(
    fields, modes, cells_ax, chunk, mode_total, rad_total, rad_size,
    where, adj, below, above, inner, outer, jac_axial, jac_radial, jac_swirl, out,
):
    lanes = adj.shape[2]
    half = modes // 2
    rad = where[1]
    lane = lax.broadcasted_iota(jnp.int32, (chunk, lanes), 1)
    row = lax.broadcasted_iota(jnp.int32, (chunk, lanes), 0)
    radius = 0.5 + ((rad * lanes + lane).astype(jnp.float32) + 0.5) / jnp.float32(2.0 * rad_total)
    swirl = 0.25 / radius
    has_inner = jnp.where((lane == 0) & (rad == 0), 0.0, 0.5)
    has_outer = jnp.where((lane == lanes - 1) & (rad == rad_size - 1), 0.0, 0.5)

    def step(i, carry):
        order = (where[0] * half + i * chunk + row).astype(jnp.float32) / jnp.float32(mode_total // 2)
        rate = swirl * order
        for p in range(2):
            halo = pl.ds(2 * i * chunk + p, chunk, stride=2)
            for x in range(cells_ax):
                def at(e, parity, cell):
                    start = (2 * i * chunk + parity) * cells_ax + cell
                    return adj[e, pl.ds(start, chunk, stride=2 * cells_ax), :]

                here = pl.ds((2 * i * chunk + p) * cells_ax + x, chunk, stride=2 * cells_ax)
                total = [None] * fields
                for e in range(fields):
                    centre = at(e, p, x)
                    low = below[e, halo, :] if x == 0 else at(e, p, x - 1)
                    high = above[e, halo, :] if x == cells_ax - 1 else at(e, p, x + 1)
                    axial = 0.5 * (high - low)
                    from_inner = jnp.where(lane == lanes - 1, inner[e, here, :], centre)
                    from_outer = jnp.where(lane == 0, outer[e, here, :], centre)
                    radial = has_outer * pltpu.roll(from_outer, lanes - 1, 1) - has_inner * pltpu.roll(
                        from_inner, 1, 1
                    )
                    turned = (rate if p == 0 else -rate) * at(e, 1 - p, x)
                    for f in range(fields):
                        term = (
                            jac_axial[e, f] * axial
                            + jac_radial[e, f] * radial
                            + jac_swirl[e, f] * turned
                        )
                        if f == e:
                            term = term + centre
                        total[f] = term if e == 0 else total[f] + term
                for f in range(fields):
                    out[f, here, :] = total[f]
        return carry

    lax.fori_loop(0, half // chunk, step, 0)


def whole(shape):
    return pl.BlockSpec(shape, lambda i, where: (0,) * len(shape))


def stepped(shape):
    return pl.BlockSpec((1, *shape[1:]), lambda i, where: (i,) + (0,) * (len(shape) - 1))


def chosen(shape):
    return pl.BlockSpec((1, *shape[1:]), lambda i, where: (where[0],) + (0,) * (len(shape) - 1))


SMEM = pl.BlockSpec(memory_space=pltpu.SMEM)
ANY = pl.BlockSpec(memory_space=pl.ANY)


def call(kernel, steps, where, args, in_specs, outs, out_specs, scratch, flops):
    moved = sum(a.size * a.dtype.itemsize for a in args) + sum(o.size * o.dtype.itemsize for o in outs)
    return pl.pallas_call(
        kernel,
        grid_spec=pltpu.PrefetchScalarGridSpec(
            num_scalar_prefetch=1,
            grid=(steps,),
            in_specs=in_specs,
            out_specs=out_specs,
            scratch_shapes=scratch,
        ),
        out_shape=outs,
        compiler_params=pltpu.CompilerParams(vmem_limit_bytes=VMEM_LIMIT),
        cost_estimate=pl.CostEstimate(flops=flops, bytes_accessed=moved, transcendentals=0),
    )(where, *args)


def body(adjoint, state, wake, jac_axial, jac_radial, jac_swirl, wake_coupling):
    fields, modes, cells_ax, lanes = adjoint.shape
    groups = lax.axis_size("mode")
    count = groups * modes
    rad_size = lax.axis_size("rad")
    ax_size = lax.axis_size("ax")
    width = 2 if cells_ax % 2 == 0 else 1
    steps = cells_ax // width
    rows = modes * cells_ax
    cols = width * fields * lanes
    f32 = jnp.float32

    def cols_of(j, f):
        return pl.ds((j * fields + f) * lanes, lanes)

    dims = (fields, modes, cells_ax, width, cols_of)
    own_table, other_table, back_table = tables(groups, modes)
    where = jnp.stack([lax.axis_index("mode"), lax.axis_index("rad")]).astype(jnp.int32)

    adj = adjoint.reshape(fields, rows, lanes)
    st = state.reshape(fields, rows, lanes)
    wk = wake.reshape(rows, lanes)

    def fetch(value, s):
        return lax.ppermute(value, "mode", [((i + s) % groups, i) for i in range(groups)])

    def deliver(value, s):
        return lax.ppermute(value, "mode", [(i, (i + s) % groups) for i in range(groups)])

    adj_recv = [fetch(adj, s) for s in range(1, groups)]

    up = [(i, i + 1) for i in range(ax_size - 1)]
    down = [(i + 1, i) for i in range(ax_size - 1)]
    below = lax.ppermute(adjoint[:, :, cells_ax - 1, :], "ax", up)
    above = lax.ppermute(adjoint[:, :, 0, :], "ax", down)
    if rad_size == 2:
        inner = outer = lax.ppermute(adj, "rad", [(0, 1), (1, 0)])
    else:
        inner = lax.ppermute(adj, "rad", [(i, i + 1) for i in range(rad_size - 1)])
        outer = lax.ppermute(adj, "rad", [(i + 1, i) for i in range(rad_size - 1)])
    wake_recv = [fetch(wk, s) for s in range(1, groups)]

    field_shape = (fields, rows, lanes)
    angle_shape = (steps, count, cols)
    angle = jax.ShapeDtypeStruct(angle_shape, f32)
    field = jax.ShapeDtypeStruct(field_shape, f32)
    plane = jax.ShapeDtypeStruct((rows, lanes), f32)
    own_flops = 2 * 2 * 3 * count * modes * steps * cols

    a_own, c_own = call(
        functools.partial(own_kernel, dims), steps, where,
        (adj, st, wake_coupling, own_table),
        [whole(field_shape), whole(field_shape), SMEM, chosen(own_table.shape)],
        [angle, angle],
        [stepped(angle_shape), stepped(angle_shape)],
        [pltpu.VMEM((3 * modes, cols), jnp.bfloat16)] * 2,
        own_flops,
    )

    chunk = 16 if modes % 32 == 0 else 8
    base = call(
        functools.partial(
            base_kernel, fields, modes, cells_ax, chunk, count, lanes * rad_size, rad_size
        ),
        1, where,
        (adj, below, above, inner, outer, jac_axial, jac_radial, jac_swirl),
        [whole(field_shape), whole(below.shape), whole(above.shape)]
        + [whole(field_shape)] * 2 + [SMEM] * 3,
        [field], [whole(field_shape)], [],
        32 * fields * fields * rows * lanes,
    )[0]

    joined = call(
        functools.partial(join_kernel, dims, groups), steps, where,
        (*adj_recv, a_own, c_own, other_table, base),
        [whole(field_shape)] * (groups - 1)
        + [stepped(angle_shape), stepped(angle_shape), chosen(other_table.shape), ANY],
        [angle] + [plane] * groups,
        [stepped(angle_shape)] + [whole((rows, lanes))] * groups,
        [pltpu.VMEM((3 * modes, cols), jnp.bfloat16)],
        (groups - 1) * own_flops // 2,
    )
    a_all, parts = joined[0], joined[1:]
    part_recv = [deliver(parts[s], s) for s in range(1, groups)]

    adjoint_in = call(
        functools.partial(back_kernel, dims, groups), steps, where,
        (wk, *wake_recv, a_all, base, wake_coupling, back_table),
        [whole((rows, lanes))] * groups
        + [stepped(angle_shape), whole(field_shape), SMEM, chosen(back_table.shape)],
        [field], [whole(field_shape)],
        [pltpu.VMEM((3 * count, cols), jnp.bfloat16)],
        own_flops // 2,
    )[0]

    total = parts[0]
    for part in part_recv:
        total = total + part
    return (
        adjoint_in.reshape(adjoint.shape),
        (-total).reshape(wake.shape),
    )


def solution(mesh):
    return jax.shard_map(
        body,
        mesh=mesh,
        in_specs=(
            P(None, "mode", "ax", "rad"),
            P(None, "mode", "ax", "rad"),
            P("mode", "ax", "rad"),
            P(),
            P(),
            P(),
            P(),
        ),
        out_specs=(P(None, "mode", "ax", "rad"), P("mode", "ax", "rad")),
        check_vma=False,
    )
```

```python
import functools
import math

import jax
import jax.numpy as jnp
import ml_dtypes
import numpy as np
from jax import lax
from jax.experimental import pallas as pl
from jax.experimental.pallas import tpu as pltpu
from jax.sharding import PartitionSpec as P

VMEM_LIMIT = 32 * 1024 * 1024


def fourier_basis(count):
    angle = np.arange(count)[:, None]
    coef = np.arange(count)[None, :]
    phase = ((coef // 2) * angle % count) * (2.0 * math.pi / count)
    table = math.sqrt(2.0 / count) * np.where(coef % 2 == 0, np.cos(phase), np.sin(phase))
    table = np.where(coef == 0, 1.0 / math.sqrt(count), table)
    table = np.where(coef == 1, np.where(angle % 2 == 0, 1.0, -1.0) / math.sqrt(count), table)
    return table.astype(np.float32)


def three_terms(table):
    high = table.astype(ml_dtypes.bfloat16)
    low = (table - high.astype(np.float32)).astype(ml_dtypes.bfloat16)
    return np.concatenate([high, low, high], axis=-1)


def tables(groups, modes_here):
    count = groups * modes_here
    basis = fourier_basis(count)
    own, other, back = [], [], []
    for m in range(groups):
        rolled = np.roll(np.roll(basis, -m * modes_here, axis=0), -m * modes_here, axis=1)
        blocks = [rolled[:, s * modes_here : (s + 1) * modes_here] for s in range(groups)]
        own.append(three_terms(blocks[0]))
        other.append(np.stack([three_terms(block) for block in blocks[1:]]))
        back.append(three_terms(np.ascontiguousarray(blocks[0].T)))
    return np.stack(own), np.stack(other), np.stack(back)


def split(value):
    high = value.astype(jnp.bfloat16)
    low = (value - high.astype(jnp.float32)).astype(jnp.bfloat16)
    return high, low


def put_split(terms, row, rows, total, cols, value):
    high, low = split(value)
    terms[pl.ds(row, rows), cols] = high
    terms[pl.ds(total + row, rows), cols] = high
    terms[pl.ds(2 * total + row, rows), cols] = low


def pack_kernel(fields, modes, cells_ax, adj, first, last, edges):
    lanes = adj.shape[2]
    lane = lax.broadcasted_iota(jnp.int32, (modes, lanes), 1)
    packed = jnp.zeros((modes, lanes), jnp.float32)
    for f in range(fields):
        for x in range(cells_ax):
            block = adj[f, pl.ds(x, modes, stride=cells_ax), :]
            if x == 0:
                first[f] = block
            if x == cells_ax - 1:
                last[f] = block
            j = f * cells_ax + x
            packed = jnp.where(lane == j, pltpu.roll(block, j, 1), packed)
            packed = jnp.where(
                lane == lanes // 2 + j, pltpu.roll(block, (j + 1 + lanes // 2) % lanes, 1), packed
            )
    edges[...] = packed


def own_kernel(dims, where, adj, state, coupling, table, a_out, c_out, terms_a, terms_c):
    fields, modes, cells_ax, width, cols_of = dims
    for j in range(width):
        x = pl.program_id(0) * width + j
        rows = pl.ds(x, modes, stride=cells_ax)
        for f in range(fields):
            put_split(terms_a, 0, modes, modes, cols_of(j, f), adj[f, rows, :])
    a_out[0] = jnp.dot(table[0], terms_a[...], preferred_element_type=jnp.float32)
    for j in range(width):
        x = pl.program_id(0) * width + j
        rows = pl.ds(x, modes, stride=cells_ax)
        for f in range(fields):
            mixed = coupling[f, 0] * state[0, rows, :]
            for e in range(1, fields):
                mixed = mixed + coupling[f, e] * state[e, rows, :]
            put_split(terms_c, 0, modes, modes, cols_of(j, f), mixed)
    c_out[0] = jnp.dot(table[0], terms_c[...], preferred_element_type=jnp.float32)


def join_kernel(dims, groups, where, *refs):
    fields, modes, cells_ax, width, cols_of = dims
    recv = refs[: groups - 1]
    a_own, c_own, table, _, a_out = refs[groups - 1 : groups + 4]
    h_out = refs[groups + 4 : 2 * groups + 4]
    terms = refs[2 * groups + 4]
    total = a_own[0]
    for s in range(groups - 1):
        for j in range(width):
            x = pl.program_id(0) * width + j
            rows = pl.ds(x, modes, stride=cells_ax)
            for f in range(fields):
                put_split(terms, 0, modes, modes, cols_of(j, f), recv[s][f, rows, :])
        total = total + jnp.dot(table[0, s], terms[...], preferred_element_type=jnp.float32)
    a_out[0] = total
    for j in range(width):
        x = pl.program_id(0) * width + j
        rows = pl.ds(x, modes, stride=cells_ax)
        for s in range(groups):
            here = pl.ds(s * modes, modes)
            part = a_out[0, here, cols_of(j, 0)] * c_own[0, here, cols_of(j, 0)]
            for f in range(1, fields):
                part = part + a_out[0, here, cols_of(j, f)] * c_own[0, here, cols_of(j, f)]
            h_out[s][rows, :] = part


def back_kernel(dims, groups, where, *refs):
    fields, modes, cells_ax, width, cols_of = dims
    wakes = refs[:groups]
    angle, base, coupling, table, out, terms = refs[groups:]
    count = groups * modes
    for j in range(width):
        x = pl.program_id(0) * width + j
        rows = pl.ds(x, modes, stride=cells_ax)
        for s in range(groups):
            wake = wakes[s][rows, :]
            for f in range(fields):
                scaled = wake * angle[0, pl.ds(s * modes, modes), cols_of(j, f)]
                put_split(terms, s * modes, modes, count, cols_of(j, f), scaled)
    returned = jnp.dot(table[0], terms[...], preferred_element_type=jnp.float32)
    for j in range(width):
        x = pl.program_id(0) * width + j
        rows = pl.ds(x, modes, stride=cells_ax)
        for f in range(fields):
            value = base[f, rows, :]
            for e in range(fields):
                value = value - coupling[e, f] * returned[:, cols_of(j, e)]
            out[f, rows, :] = value


def base_kernel(
    fields, modes, cells_ax, chunk, mode_total, rad_total, rad_size,
    where, adj, below, above, inner, outer, jac_axial, jac_radial, jac_swirl, out,
):
    lanes = adj.shape[2]
    half = modes // 2
    rad = where[1]
    lane = lax.broadcasted_iota(jnp.int32, (chunk, lanes), 1)
    row = lax.broadcasted_iota(jnp.int32, (chunk, lanes), 0)
    radius = 0.5 + ((rad * lanes + lane).astype(jnp.float32) + 0.5) / jnp.float32(2.0 * rad_total)
    swirl = 0.25 / radius
    has_inner = jnp.where((lane == 0) & (rad == 0), 0.0, 0.5)
    has_outer = jnp.where((lane == lanes - 1) & (rad == rad_size - 1), 0.0, 0.5)

    def step(i, carry):
        order = (where[0] * half + i * chunk + row).astype(jnp.float32) / jnp.float32(mode_total // 2)
        rate = swirl * order
        for p in range(2):
            halo = pl.ds(2 * i * chunk + p, chunk, stride=2)
            inner_edges, outer_edges = inner[halo, :], outer[halo, :]
            for x in range(cells_ax):
                def at(e, parity, cell):
                    start = (2 * i * chunk + parity) * cells_ax + cell
                    return adj[e, pl.ds(start, chunk, stride=2 * cells_ax), :]

                here = pl.ds((2 * i * chunk + p) * cells_ax + x, chunk, stride=2 * cells_ax)
                total = [None] * fields
                for e in range(fields):
                    centre = at(e, p, x)
                    low = below[e, halo, :] if x == 0 else at(e, p, x - 1)
                    high = above[e, halo, :] if x == cells_ax - 1 else at(e, p, x + 1)
                    axial = 0.5 * (high - low)
                    j = e * cells_ax + x
                    from_inner = jnp.where(
                        lane == lanes - 1, pltpu.roll(inner_edges, lanes // 2 - 1 - j, 1), centre
                    )
                    from_outer = jnp.where(
                        lane == 0, pltpu.roll(outer_edges, (lanes - j) % lanes, 1), centre
                    )
                    radial = has_outer * pltpu.roll(from_outer, lanes - 1, 1) - has_inner * pltpu.roll(
                        from_inner, 1, 1
                    )
                    turned = (rate if p == 0 else -rate) * at(e, 1 - p, x)
                    for f in range(fields):
                        term = (
                            jac_axial[e, f] * axial
                            + jac_radial[e, f] * radial
                            + jac_swirl[e, f] * turned
                        )
                        if f == e:
                            term = term + centre
                        total[f] = term if e == 0 else total[f] + term
                for f in range(fields):
                    out[f, here, :] = total[f]
        return carry

    lax.fori_loop(0, half // chunk, step, 0)


def whole(shape):
    return pl.BlockSpec(shape, lambda i, where: (0,) * len(shape))


def stepped(shape):
    return pl.BlockSpec((1, *shape[1:]), lambda i, where: (i,) + (0,) * (len(shape) - 1))


def chosen(shape):
    return pl.BlockSpec((1, *shape[1:]), lambda i, where: (where[0],) + (0,) * (len(shape) - 1))


SMEM = pl.BlockSpec(memory_space=pltpu.SMEM)
ANY = pl.BlockSpec(memory_space=pl.ANY)


def call(kernel, steps, where, args, in_specs, outs, out_specs, scratch, flops):
    moved = sum(a.size * a.dtype.itemsize for a in args) + sum(o.size * o.dtype.itemsize for o in outs)
    return pl.pallas_call(
        kernel,
        grid_spec=pltpu.PrefetchScalarGridSpec(
            num_scalar_prefetch=1,
            grid=(steps,),
            in_specs=in_specs,
            out_specs=out_specs,
            scratch_shapes=scratch,
        ),
        out_shape=outs,
        compiler_params=pltpu.CompilerParams(vmem_limit_bytes=VMEM_LIMIT),
        cost_estimate=pl.CostEstimate(flops=flops, bytes_accessed=moved, transcendentals=0),
    )(where, *args)


def body(adjoint, state, wake, jac_axial, jac_radial, jac_swirl, wake_coupling):
    fields, modes, cells_ax, lanes = adjoint.shape
    groups = lax.axis_size("mode")
    count = groups * modes
    rad_size = lax.axis_size("rad")
    ax_size = lax.axis_size("ax")
    width = 2 if cells_ax % 2 == 0 else 1
    steps = cells_ax // width
    rows = modes * cells_ax
    cols = width * fields * lanes
    f32 = jnp.float32

    def cols_of(j, f):
        return pl.ds((j * fields + f) * lanes, lanes)

    dims = (fields, modes, cells_ax, width, cols_of)
    own_table, other_table, back_table = tables(groups, modes)
    where = jnp.stack([lax.axis_index("mode"), lax.axis_index("rad")]).astype(jnp.int32)

    adj = adjoint.reshape(fields, rows, lanes)
    st = state.reshape(fields, rows, lanes)
    wk = wake.reshape(rows, lanes)

    def fetch(value, s):
        return lax.ppermute(value, "mode", [((i + s) % groups, i) for i in range(groups)])

    def deliver(value, s):
        return lax.ppermute(value, "mode", [(i, (i + s) % groups) for i in range(groups)])

    adj_recv = [fetch(adj, s) for s in range(1, groups)]

    up = [(i, i + 1) for i in range(ax_size - 1)]
    down = [(i + 1, i) for i in range(ax_size - 1)]
    layer = jax.ShapeDtypeStruct((fields, modes, lanes), adjoint.dtype)
    first, last, edges = pl.pallas_call(
        functools.partial(pack_kernel, fields, modes, cells_ax),
        out_shape=[layer, layer, jax.ShapeDtypeStruct((modes, lanes), adjoint.dtype)],
        compiler_params=pltpu.CompilerParams(vmem_limit_bytes=VMEM_LIMIT),
    )(adj)
    below = lax.ppermute(last, "ax", up)
    above = lax.ppermute(first, "ax", down)
    if rad_size == 2:
        inner = outer = lax.ppermute(edges, "rad", [(0, 1), (1, 0)])
    else:
        inner = lax.ppermute(edges, "rad", [(i, i + 1) for i in range(rad_size - 1)])
        outer = lax.ppermute(edges, "rad", [(i + 1, i) for i in range(rad_size - 1)])
    wake_recv = [fetch(wk, s) for s in range(1, groups)]

    field_shape = (fields, rows, lanes)
    angle_shape = (steps, count, cols)
    angle = jax.ShapeDtypeStruct(angle_shape, f32)
    field = jax.ShapeDtypeStruct(field_shape, f32)
    plane = jax.ShapeDtypeStruct((rows, lanes), f32)
    own_flops = 2 * 2 * 3 * count * modes * steps * cols

    a_own, c_own = call(
        functools.partial(own_kernel, dims), steps, where,
        (adj, st, wake_coupling, own_table),
        [whole(field_shape), whole(field_shape), SMEM, chosen(own_table.shape)],
        [angle, angle],
        [stepped(angle_shape), stepped(angle_shape)],
        [pltpu.VMEM((3 * modes, cols), jnp.bfloat16)] * 2,
        own_flops,
    )

    chunk = 16 if modes % 32 == 0 else 8
    base = call(
        functools.partial(
            base_kernel, fields, modes, cells_ax, chunk, count, lanes * rad_size, rad_size
        ),
        1, where,
        (adj, below, above, inner, outer, jac_axial, jac_radial, jac_swirl),
        [whole(field_shape), whole(below.shape), whole(above.shape)]
        + [whole(edges.shape)] * 2 + [SMEM] * 3,
        [field], [whole(field_shape)], [],
        32 * fields * fields * rows * lanes,
    )[0]

    joined = call(
        functools.partial(join_kernel, dims, groups), steps, where,
        (*adj_recv, a_own, c_own, other_table, base),
        [whole(field_shape)] * (groups - 1)
        + [stepped(angle_shape), stepped(angle_shape), chosen(other_table.shape), ANY],
        [angle] + [plane] * groups,
        [stepped(angle_shape)] + [whole((rows, lanes))] * groups,
        [pltpu.VMEM((3 * modes, cols), jnp.bfloat16)],
        (groups - 1) * own_flops // 2,
    )
    a_all, parts = joined[0], joined[1:]
    part_recv = [deliver(parts[s], s) for s in range(1, groups)]

    adjoint_in = call(
        functools.partial(back_kernel, dims, groups), steps, where,
        (wk, *wake_recv, a_all, base, wake_coupling, back_table),
        [whole((rows, lanes))] * groups
        + [stepped(angle_shape), whole(field_shape), SMEM, chosen(back_table.shape)],
        [field], [whole(field_shape)],
        [pltpu.VMEM((3 * count, cols), jnp.bfloat16)],
        own_flops // 2,
    )[0]

    total = parts[0]
    for part in part_recv:
        total = total + part
    return (
        adjoint_in.reshape(adjoint.shape),
        (-total).reshape(wake.shape),
    )


def solution(mesh):
    return jax.shard_map(
        body,
        mesh=mesh,
        in_specs=(
            P(None, "mode", "ax", "rad"),
            P(None, "mode", "ax", "rad"),
            P("mode", "ax", "rad"),
            P(),
            P(),
            P(),
            P(),
        ),
        out_specs=(P(None, "mode", "ax", "rad"), P("mode", "ax", "rad")),
        check_vma=False,
    )
```

```python
import functools
import math

import jax
import jax.numpy as jnp
import ml_dtypes
import numpy as np
from jax import lax
from jax.experimental import pallas as pl
from jax.experimental.pallas import tpu as pltpu
from jax.sharding import PartitionSpec as P

VMEM_LIMIT = 32 * 1024 * 1024


def fourier_basis(count):
    angle = np.arange(count)[:, None]
    coef = np.arange(count)[None, :]
    phase = ((coef // 2) * angle % count) * (2.0 * math.pi / count)
    table = math.sqrt(2.0 / count) * np.where(coef % 2 == 0, np.cos(phase), np.sin(phase))
    table = np.where(coef == 0, 1.0 / math.sqrt(count), table)
    table = np.where(coef == 1, np.where(angle % 2 == 0, 1.0, -1.0) / math.sqrt(count), table)
    return table.astype(np.float32)


def three_terms(table):
    high = table.astype(ml_dtypes.bfloat16)
    low = (table - high.astype(np.float32)).astype(ml_dtypes.bfloat16)
    return np.concatenate([high, low, high], axis=-1)


def tables(groups, modes_here):
    count = groups * modes_here
    basis = fourier_basis(count)
    own, other, back = [], [], []
    for m in range(groups):
        rolled = np.roll(np.roll(basis, -m * modes_here, axis=0), -m * modes_here, axis=1)
        blocks = [rolled[:, s * modes_here : (s + 1) * modes_here] for s in range(groups)]
        own.append(three_terms(blocks[0]))
        other.append(np.stack([three_terms(block) for block in blocks[1:]]))
        back.append(three_terms(np.ascontiguousarray(blocks[0].T)))
    return np.stack(own), np.stack(other), np.stack(back)


def split(value):
    high = value.astype(jnp.bfloat16)
    low = (value - high.astype(jnp.float32)).astype(jnp.bfloat16)
    return high, low


def put_split(terms, row, rows, total, cols, value):
    high, low = split(value)
    terms[pl.ds(row, rows), cols] = high
    terms[pl.ds(total + row, rows), cols] = high
    terms[pl.ds(2 * total + row, rows), cols] = low


def pack_kernel(fields, modes, cells_ax, adj, first, last, edges):
    lanes = adj.shape[2]
    lane = lax.broadcasted_iota(jnp.int32, (modes, lanes), 1)
    packed = jnp.zeros((modes, lanes), jnp.float32)
    for f in range(fields):
        for x in range(cells_ax):
            block = adj[f, pl.ds(x, modes, stride=cells_ax), :]
            if x == 0:
                first[f] = block
            if x == cells_ax - 1:
                last[f] = block
            j = f * cells_ax + x
            packed = jnp.where(lane == j, pltpu.roll(block, j, 1), packed)
            packed = jnp.where(
                lane == lanes // 2 + j, pltpu.roll(block, (j + 1 + lanes // 2) % lanes, 1), packed
            )
    edges[...] = packed


def own_kernel(dims, where, adj, state, coupling, table, a_out, c_out, terms_a, terms_c):
    fields, modes, cells_ax, width, cols_of = dims
    for j in range(width):
        x = pl.program_id(0) * width + j
        rows = pl.ds(x, modes, stride=cells_ax)
        for f in range(fields):
            put_split(terms_a, 0, modes, modes, cols_of(j, f), adj[f, rows, :])
    a_out[0] = jnp.dot(table[0], terms_a[...], preferred_element_type=jnp.float32)
    for j in range(width):
        x = pl.program_id(0) * width + j
        rows = pl.ds(x, modes, stride=cells_ax)
        for f in range(fields):
            mixed = coupling[f, 0] * state[0, rows, :]
            for e in range(1, fields):
                mixed = mixed + coupling[f, e] * state[e, rows, :]
            put_split(terms_c, 0, modes, modes, cols_of(j, f), mixed)
    c_out[0] = jnp.dot(table[0], terms_c[...], preferred_element_type=jnp.float32)


def join_kernel(dims, groups, cuts, where, *refs):
    fields, modes, cells_ax, width, cols_of = dims
    pieces = len(cuts) - 1
    recv = refs[: groups - 1]
    a_own, c_own, table, _, a_out = refs[groups - 1 : groups + 4]
    h_out = refs[groups + 4 : -1]
    terms = refs[-1]
    total = a_own[0]
    for s in range(groups - 1):
        for j in range(width):
            x = pl.program_id(0) * width + j
            rows = pl.ds(x, modes, stride=cells_ax)
            for f in range(fields):
                put_split(terms, 0, modes, modes, cols_of(j, f), recv[s][f, rows, :])
        total = total + jnp.dot(table[0, s], terms[...], preferred_element_type=jnp.float32)
    a_out[0] = total
    for j in range(width):
        x = pl.program_id(0) * width + j
        for s, k in ((s, k) for s in range(groups) for k in range(pieces)):
            here = pl.ds(s * modes + cuts[k], cuts[k + 1] - cuts[k])
            rows = pl.ds(x, cuts[k + 1] - cuts[k], stride=cells_ax)
            part = a_out[0, here, cols_of(j, 0)] * c_own[0, here, cols_of(j, 0)]
            for f in range(1, fields):
                part = part + a_out[0, here, cols_of(j, f)] * c_own[0, here, cols_of(j, f)]
            h_out[s * pieces + k][rows, :] = part


def total_kernel(terms, *refs):
    total = refs[0][...]
    for ref in refs[1:terms]:
        total = total + ref[...]
    refs[-1][...] = -total


def back_kernel(dims, groups, where, *refs):
    fields, modes, cells_ax, width, cols_of = dims
    wakes = refs[:groups]
    angle, base, coupling, table, out, terms = refs[groups:]
    count = groups * modes
    for j in range(width):
        x = pl.program_id(0) * width + j
        rows = pl.ds(x, modes, stride=cells_ax)
        for s in range(groups):
            wake = wakes[s][rows, :]
            for f in range(fields):
                scaled = wake * angle[0, pl.ds(s * modes, modes), cols_of(j, f)]
                put_split(terms, s * modes, modes, count, cols_of(j, f), scaled)
    returned = jnp.dot(table[0], terms[...], preferred_element_type=jnp.float32)
    for j in range(width):
        x = pl.program_id(0) * width + j
        rows = pl.ds(x, modes, stride=cells_ax)
        for f in range(fields):
            value = base[f, rows, :]
            for e in range(fields):
                value = value - coupling[e, f] * returned[:, cols_of(j, e)]
            out[f, rows, :] = value


def base_kernel(
    fields, modes, cells_ax, chunk, mode_total, rad_total, rad_size,
    where, adj, below, above, inner, outer, jac_axial, jac_radial, jac_swirl, out,
):
    lanes = adj.shape[2]
    half = modes // 2
    rad = where[1]
    lane = lax.broadcasted_iota(jnp.int32, (chunk, lanes), 1)
    row = lax.broadcasted_iota(jnp.int32, (chunk, lanes), 0)
    radius = 0.5 + ((rad * lanes + lane).astype(jnp.float32) + 0.5) / jnp.float32(2.0 * rad_total)
    swirl = 0.25 / radius
    has_inner = jnp.where((lane == 0) & (rad == 0), 0.0, 0.5)
    has_outer = jnp.where((lane == lanes - 1) & (rad == rad_size - 1), 0.0, 0.5)

    def step(i, carry):
        order = (where[0] * half + i * chunk + row).astype(jnp.float32) / jnp.float32(mode_total // 2)
        rate = swirl * order
        for p in range(2):
            halo = pl.ds(2 * i * chunk + p, chunk, stride=2)
            inner_edges, outer_edges = inner[halo, :], outer[halo, :]
            for x in range(cells_ax):
                def at(e, parity, cell):
                    start = (2 * i * chunk + parity) * cells_ax + cell
                    return adj[e, pl.ds(start, chunk, stride=2 * cells_ax), :]

                here = pl.ds((2 * i * chunk + p) * cells_ax + x, chunk, stride=2 * cells_ax)
                total = [None] * fields
                for e in range(fields):
                    centre = at(e, p, x)
                    low = below[e, halo, :] if x == 0 else at(e, p, x - 1)
                    high = above[e, halo, :] if x == cells_ax - 1 else at(e, p, x + 1)
                    axial = 0.5 * (high - low)
                    j = e * cells_ax + x
                    from_inner = jnp.where(
                        lane == lanes - 1, pltpu.roll(inner_edges, lanes // 2 - 1 - j, 1), centre
                    )
                    from_outer = jnp.where(
                        lane == 0, pltpu.roll(outer_edges, (lanes - j) % lanes, 1), centre
                    )
                    radial = has_outer * pltpu.roll(from_outer, lanes - 1, 1) - has_inner * pltpu.roll(
                        from_inner, 1, 1
                    )
                    turned = (rate if p == 0 else -rate) * at(e, 1 - p, x)
                    for f in range(fields):
                        term = (
                            jac_axial[e, f] * axial
                            + jac_radial[e, f] * radial
                            + jac_swirl[e, f] * turned
                        )
                        if f == e:
                            term = term + centre
                        total[f] = term if e == 0 else total[f] + term
                for f in range(fields):
                    out[f, here, :] = total[f]
        return carry

    lax.fori_loop(0, half // chunk, step, 0)


def whole(shape):
    return pl.BlockSpec(shape, lambda i, where: (0,) * len(shape))


def stepped(shape):
    return pl.BlockSpec((1, *shape[1:]), lambda i, where: (i,) + (0,) * (len(shape) - 1))


def chosen(shape):
    return pl.BlockSpec((1, *shape[1:]), lambda i, where: (where[0],) + (0,) * (len(shape) - 1))


SMEM = pl.BlockSpec(memory_space=pltpu.SMEM)
ANY = pl.BlockSpec(memory_space=pl.ANY)


def call(kernel, steps, where, args, in_specs, outs, out_specs, scratch, flops):
    moved = sum(a.size * a.dtype.itemsize for a in args) + sum(o.size * o.dtype.itemsize for o in outs)
    return pl.pallas_call(
        kernel,
        grid_spec=pltpu.PrefetchScalarGridSpec(
            num_scalar_prefetch=1,
            grid=(steps,),
            in_specs=in_specs,
            out_specs=out_specs,
            scratch_shapes=scratch,
        ),
        out_shape=outs,
        compiler_params=pltpu.CompilerParams(vmem_limit_bytes=VMEM_LIMIT),
        cost_estimate=pl.CostEstimate(flops=flops, bytes_accessed=moved, transcendentals=0),
    )(where, *args)


def body(adjoint, state, wake, jac_axial, jac_radial, jac_swirl, wake_coupling):
    fields, modes, cells_ax, lanes = adjoint.shape
    groups = lax.axis_size("mode")
    count = groups * modes
    rad_size = lax.axis_size("rad")
    ax_size = lax.axis_size("ax")
    width = 2 if cells_ax % 2 == 0 else 1
    steps = cells_ax // width
    rows = modes * cells_ax
    cols = width * fields * lanes
    f32 = jnp.float32

    def cols_of(j, f):
        return pl.ds((j * fields + f) * lanes, lanes)

    dims = (fields, modes, cells_ax, width, cols_of)
    own_table, other_table, back_table = tables(groups, modes)
    where = jnp.stack([lax.axis_index("mode"), lax.axis_index("rad")]).astype(jnp.int32)

    adj = adjoint.reshape(fields, rows, lanes)
    st = state.reshape(fields, rows, lanes)
    wk = wake.reshape(rows, lanes)

    def fetch(value, s):
        return lax.ppermute(value, "mode", [((i + s) % groups, i) for i in range(groups)])

    def deliver(value, s):
        return lax.ppermute(value, "mode", [(i, (i + s) % groups) for i in range(groups)])

    adj_recv = [fetch(adj, s) for s in range(1, groups)]

    up = [(i, i + 1) for i in range(ax_size - 1)]
    down = [(i + 1, i) for i in range(ax_size - 1)]
    layer = jax.ShapeDtypeStruct((fields, modes, lanes), adjoint.dtype)
    first, last, edges = pl.pallas_call(
        functools.partial(pack_kernel, fields, modes, cells_ax),
        out_shape=[layer, layer, jax.ShapeDtypeStruct((modes, lanes), adjoint.dtype)],
        compiler_params=pltpu.CompilerParams(vmem_limit_bytes=VMEM_LIMIT),
    )(adj)
    below = lax.ppermute(last, "ax", up)
    above = lax.ppermute(first, "ax", down)
    if rad_size == 2:
        inner = outer = lax.ppermute(edges, "rad", [(0, 1), (1, 0)])
    else:
        inner = lax.ppermute(edges, "rad", [(i, i + 1) for i in range(rad_size - 1)])
        outer = lax.ppermute(edges, "rad", [(i + 1, i) for i in range(rad_size - 1)])
    wake_recv = [fetch(wk, s) for s in range(1, groups)]

    field_shape = (fields, rows, lanes)
    angle_shape = (steps, count, cols)
    angle = jax.ShapeDtypeStruct(angle_shape, f32)
    field = jax.ShapeDtypeStruct(field_shape, f32)
    plane = jax.ShapeDtypeStruct((rows, lanes), f32)
    own_flops = 2 * 2 * 3 * count * modes * steps * cols

    a_own, c_own = call(
        functools.partial(own_kernel, dims), steps, where,
        (adj, st, wake_coupling, own_table),
        [whole(field_shape), whole(field_shape), SMEM, chosen(own_table.shape)],
        [angle, angle],
        [stepped(angle_shape), stepped(angle_shape)],
        [pltpu.VMEM((3 * modes, cols), jnp.bfloat16)] * 2,
        own_flops,
    )

    chunk = 16 if modes % 32 == 0 else 8
    base = call(
        functools.partial(
            base_kernel, fields, modes, cells_ax, chunk, count, lanes * rad_size, rad_size
        ),
        1, where,
        (adj, below, above, inner, outer, jac_axial, jac_radial, jac_swirl),
        [whole(field_shape), whole(below.shape), whole(above.shape)]
        + [whole(edges.shape)] * 2 + [SMEM] * 3,
        [field], [whole(field_shape)], [],
        32 * fields * fields * rows * lanes,
    )[0]

    cuts = (0, max(modes * 3 // 4 // 8 * 8, modes // 2), modes)
    pieces = len(cuts) - 1
    piece_rows = [(cuts[k + 1] - cuts[k]) * cells_ax for k in range(pieces)]
    joined = call(
        functools.partial(join_kernel, dims, groups, cuts), steps, where,
        (*adj_recv, a_own, c_own, other_table, base),
        [whole(field_shape)] * (groups - 1)
        + [stepped(angle_shape), stepped(angle_shape), chosen(other_table.shape), ANY],
        [angle] + [jax.ShapeDtypeStruct((n, lanes), f32) for n in piece_rows] * groups,
        [stepped(angle_shape)] + [whole((n, lanes)) for n in piece_rows] * groups,
        [pltpu.VMEM((3 * modes, cols), jnp.bfloat16)],
        (groups - 1) * own_flops // 2,
    )
    a_all = joined[0]
    parts = [joined[1 + k :: pieces] for k in range(pieces)]
    arrived = [[deliver(part[s], s) for s in range(1, groups)] for part in parts]

    adjoint_in = call(
        functools.partial(back_kernel, dims, groups), steps, where,
        (wk, *wake_recv, a_all, base, wake_coupling, back_table),
        [whole((rows, lanes))] * groups
        + [stepped(angle_shape), whole(field_shape), SMEM, chosen(back_table.shape)],
        [field], [whole(field_shape)],
        [pltpu.VMEM((3 * count, cols), jnp.bfloat16)],
        own_flops // 2,
    )[0]

    wake_grad = None
    for k in range(pieces):
        size, place = piece_rows[k], cuts[k] * cells_ax
        wake_grad = pl.pallas_call(
            functools.partial(total_kernel, groups),
            grid=(1,),
            out_shape=plane,
            in_specs=[pl.BlockSpec((size, lanes), lambda i: (0, 0))] * groups
            + ([] if wake_grad is None else [ANY]),
            out_specs=pl.BlockSpec((size, lanes), lambda i, at=place // size: (at, 0)),
            input_output_aliases={} if wake_grad is None else {groups: 0},
            compiler_params=pltpu.CompilerParams(vmem_limit_bytes=VMEM_LIMIT),
        )(parts[k][0], *arrived[k], *([] if wake_grad is None else [wake_grad]))
    return (
        adjoint_in.reshape(adjoint.shape),
        wake_grad.reshape(wake.shape),
    )


def solution(mesh):
    return jax.shard_map(
        body,
        mesh=mesh,
        in_specs=(
            P(None, "mode", "ax", "rad"),
            P(None, "mode", "ax", "rad"),
            P("mode", "ax", "rad"),
            P(),
            P(),
            P(),
            P(),
        ),
        out_specs=(P(None, "mode", "ax", "rad"), P("mode", "ax", "rad")),
        check_vma=False,
    )
```

```python
import functools
import math

import jax
import jax.numpy as jnp
import ml_dtypes
import numpy as np
from jax import lax
from jax.experimental import pallas as pl
from jax.experimental.pallas import tpu as pltpu
from jax.sharding import PartitionSpec as P

VMEM_LIMIT = 32 * 1024 * 1024


def fourier_basis(count):
    angle = np.arange(count)[:, None]
    coef = np.arange(count)[None, :]
    phase = ((coef // 2) * angle % count) * (2.0 * math.pi / count)
    table = math.sqrt(2.0 / count) * np.where(coef % 2 == 0, np.cos(phase), np.sin(phase))
    table = np.where(coef == 0, 1.0 / math.sqrt(count), table)
    table = np.where(coef == 1, np.where(angle % 2 == 0, 1.0, -1.0) / math.sqrt(count), table)
    return table.astype(np.float32)


def three_terms(table):
    high = table.astype(ml_dtypes.bfloat16)
    low = (table - high.astype(np.float32)).astype(ml_dtypes.bfloat16)
    return np.concatenate([high, low, high], axis=-1)


def tables(groups, modes_here):
    count = groups * modes_here
    basis = fourier_basis(count)
    own, other, back = [], [], []
    for m in range(groups):
        rolled = np.roll(np.roll(basis, -m * modes_here, axis=0), -m * modes_here, axis=1)
        blocks = [rolled[:, s * modes_here : (s + 1) * modes_here] for s in range(groups)]
        own.append(three_terms(blocks[0]))
        other.append(np.stack([three_terms(block) for block in blocks[1:]]))
        back.append(three_terms(np.ascontiguousarray(blocks[0].T)))
    return np.stack(own), np.stack(other), np.stack(back)


def split(value):
    high = value.astype(jnp.bfloat16)
    low = (value - high.astype(jnp.float32)).astype(jnp.bfloat16)
    return high, low


def put_split(terms, row, rows, total, cols, value):
    high, low = split(value)
    terms[pl.ds(row, rows), cols] = high
    terms[pl.ds(total + row, rows), cols] = high
    terms[pl.ds(2 * total + row, rows), cols] = low


def pack_kernel(fields, modes, cells_ax, adj, first, last, edges):
    lanes = adj.shape[2]
    pair = lax.broadcasted_iota(jnp.int32, (modes, lanes), 1) // 2
    packed = jnp.zeros((modes, lanes), jnp.float32)
    for f in range(fields):
        for x in range(cells_ax):
            block = adj[f, pl.ds(x, modes, stride=cells_ax), :]
            if x == 0:
                first[f] = block
            if x == cells_ax - 1:
                last[f] = block
            j = f * cells_ax + x
            packed = jnp.where(pair == j, pltpu.roll(block, 2 * j + 1, 1), packed)
    edges[...] = packed


def own_kernel(dims, where, adj, state, coupling, table, a_out, c_out, terms_a, terms_c):
    fields, modes, cells_ax, width, cols_of = dims
    for j in range(width):
        x = pl.program_id(0) * width + j
        rows = pl.ds(x, modes, stride=cells_ax)
        for f in range(fields):
            put_split(terms_a, 0, modes, modes, cols_of(j, f), adj[f, rows, :])
    a_out[0] = jnp.dot(table[0], terms_a[...], preferred_element_type=jnp.float32)
    for j in range(width):
        x = pl.program_id(0) * width + j
        rows = pl.ds(x, modes, stride=cells_ax)
        for f in range(fields):
            mixed = coupling[f, 0] * state[0, rows, :]
            for e in range(1, fields):
                mixed = mixed + coupling[f, e] * state[e, rows, :]
            put_split(terms_c, 0, modes, modes, cols_of(j, f), mixed)
    c_out[0] = jnp.dot(table[0], terms_c[...], preferred_element_type=jnp.float32)


def join_kernel(dims, groups, where, *refs):
    fields, modes, cells_ax, width, cols_of = dims
    recv = refs[: groups - 1]
    a_own, c_own, table, _, a_out = refs[groups - 1 : groups + 4]
    h_out = refs[groups + 4 : 2 * groups + 4]
    terms = refs[2 * groups + 4]
    total = a_own[0]
    for s in range(groups - 1):
        for j in range(width):
            x = pl.program_id(0) * width + j
            rows = pl.ds(x, modes, stride=cells_ax)
            for f in range(fields):
                put_split(terms, 0, modes, modes, cols_of(j, f), recv[s][f, rows, :])
        total = total + jnp.dot(table[0, s], terms[...], preferred_element_type=jnp.float32)
    a_out[0] = total
    for j in range(width):
        x = pl.program_id(0) * width + j
        rows = pl.ds(x, modes, stride=cells_ax)
        for s in range(groups):
            here = pl.ds(s * modes, modes)
            part = a_out[0, here, cols_of(j, 0)] * c_own[0, here, cols_of(j, 0)]
            for f in range(1, fields):
                part = part + a_out[0, here, cols_of(j, f)] * c_own[0, here, cols_of(j, f)]
            h_out[s][rows, :] = part


def back_kernel(dims, groups, where, *refs):
    fields, modes, cells_ax, width, cols_of = dims
    wakes = refs[:groups]
    angle, base, coupling, table, out, terms = refs[groups:]
    count = groups * modes
    for j in range(width):
        x = pl.program_id(0) * width + j
        rows = pl.ds(x, modes, stride=cells_ax)
        for s in range(groups):
            wake = wakes[s][rows, :]
            for f in range(fields):
                scaled = wake * angle[0, pl.ds(s * modes, modes), cols_of(j, f)]
                put_split(terms, s * modes, modes, count, cols_of(j, f), scaled)
    returned = jnp.dot(table[0], terms[...], preferred_element_type=jnp.float32)
    for j in range(width):
        x = pl.program_id(0) * width + j
        rows = pl.ds(x, modes, stride=cells_ax)
        for f in range(fields):
            value = base[f, rows, :]
            for e in range(fields):
                value = value - coupling[e, f] * returned[:, cols_of(j, e)]
            out[f, rows, :] = value


def base_kernel(
    fields, modes, cells_ax, chunk, mode_total, rad_total, rad_size,
    where, adj, below, above, inner, outer, jac_axial, jac_radial, jac_swirl, out,
):
    lanes = adj.shape[2]
    half = modes // 2
    rad = where[1]
    lane = lax.broadcasted_iota(jnp.int32, (chunk, lanes), 1)
    row = lax.broadcasted_iota(jnp.int32, (chunk, lanes), 0)
    radius = 0.5 + ((rad * lanes + lane).astype(jnp.float32) + 0.5) / jnp.float32(2.0 * rad_total)
    swirl = 0.25 / radius
    has_inner = jnp.where((lane == 0) & (rad == 0), 0.0, 0.5)
    has_outer = jnp.where((lane == lanes - 1) & (rad == rad_size - 1), 0.0, 0.5)

    def step(i, carry):
        order = (where[0] * half + i * chunk + row).astype(jnp.float32) / jnp.float32(mode_total // 2)
        rate = swirl * order
        for p in range(2):
            halo = pl.ds(2 * i * chunk + p, chunk, stride=2)
            edges = jnp.where(lane % 2 == 0, pltpu.roll(inner[halo, :], 2, 1), outer[halo, :])
            for x in range(cells_ax):
                def at(e, parity, cell):
                    start = (2 * i * chunk + parity) * cells_ax + cell
                    return adj[e, pl.ds(start, chunk, stride=2 * cells_ax), :]

                here = pl.ds((2 * i * chunk + p) * cells_ax + x, chunk, stride=2 * cells_ax)
                total = [None] * fields
                for e in range(fields):
                    centre = at(e, p, x)
                    low = below[e, halo, :] if x == 0 else at(e, p, x - 1)
                    high = above[e, halo, :] if x == cells_ax - 1 else at(e, p, x + 1)
                    axial = 0.5 * (high - low)
                    edge = pltpu.roll(edges, lanes - 2 * (e * cells_ax + x) - 2, 1)
                    inward = jnp.where(lane == 0, edge, pltpu.roll(centre, 1, 1))
                    outward = jnp.where(lane == lanes - 1, edge, pltpu.roll(centre, lanes - 1, 1))
                    radial = has_outer * outward - has_inner * inward
                    turned = (rate if p == 0 else -rate) * at(e, 1 - p, x)
                    for f in range(fields):
                        term = (
                            jac_axial[e, f] * axial
                            + jac_radial[e, f] * radial
                            + jac_swirl[e, f] * turned
                        )
                        if f == e:
                            term = term + centre
                        total[f] = term if e == 0 else total[f] + term
                for f in range(fields):
                    out[f, here, :] = total[f]
        return carry

    lax.fori_loop(0, half // chunk, step, 0)


def whole(shape):
    return pl.BlockSpec(shape, lambda i, where: (0,) * len(shape))


def stepped(shape):
    return pl.BlockSpec((1, *shape[1:]), lambda i, where: (i,) + (0,) * (len(shape) - 1))


def chosen(shape):
    return pl.BlockSpec((1, *shape[1:]), lambda i, where: (where[0],) + (0,) * (len(shape) - 1))


SMEM = pl.BlockSpec(memory_space=pltpu.SMEM)
ANY = pl.BlockSpec(memory_space=pl.ANY)


def call(kernel, steps, where, args, in_specs, outs, out_specs, scratch, flops):
    moved = sum(a.size * a.dtype.itemsize for a in args) + sum(o.size * o.dtype.itemsize for o in outs)
    return pl.pallas_call(
        kernel,
        grid_spec=pltpu.PrefetchScalarGridSpec(
            num_scalar_prefetch=1,
            grid=(steps,),
            in_specs=in_specs,
            out_specs=out_specs,
            scratch_shapes=scratch,
        ),
        out_shape=outs,
        compiler_params=pltpu.CompilerParams(vmem_limit_bytes=VMEM_LIMIT),
        cost_estimate=pl.CostEstimate(flops=flops, bytes_accessed=moved, transcendentals=0),
    )(where, *args)


def body(adjoint, state, wake, jac_axial, jac_radial, jac_swirl, wake_coupling):
    fields, modes, cells_ax, lanes = adjoint.shape
    groups = lax.axis_size("mode")
    count = groups * modes
    rad_size = lax.axis_size("rad")
    ax_size = lax.axis_size("ax")
    width = 2 if cells_ax % 2 == 0 else 1
    steps = cells_ax // width
    rows = modes * cells_ax
    cols = width * fields * lanes
    f32 = jnp.float32

    def cols_of(j, f):
        return pl.ds((j * fields + f) * lanes, lanes)

    dims = (fields, modes, cells_ax, width, cols_of)
    own_table, other_table, back_table = tables(groups, modes)
    where = jnp.stack([lax.axis_index("mode"), lax.axis_index("rad")]).astype(jnp.int32)

    adj = adjoint.reshape(fields, rows, lanes)
    st = state.reshape(fields, rows, lanes)
    wk = wake.reshape(rows, lanes)

    def fetch(value, s):
        return lax.ppermute(value, "mode", [((i + s) % groups, i) for i in range(groups)])

    def deliver(value, s):
        return lax.ppermute(value, "mode", [(i, (i + s) % groups) for i in range(groups)])

    adj_recv = [fetch(adj, s) for s in range(1, groups)]

    up = [(i, i + 1) for i in range(ax_size - 1)]
    down = [(i + 1, i) for i in range(ax_size - 1)]
    layer = jax.ShapeDtypeStruct((fields, modes, lanes), adjoint.dtype)
    first, last, edges = pl.pallas_call(
        functools.partial(pack_kernel, fields, modes, cells_ax),
        out_shape=[layer, layer, jax.ShapeDtypeStruct((modes, lanes), adjoint.dtype)],
        compiler_params=pltpu.CompilerParams(vmem_limit_bytes=VMEM_LIMIT),
    )(adj)
    below = lax.ppermute(last, "ax", up)
    above = lax.ppermute(first, "ax", down)
    if rad_size == 2:
        inner = outer = lax.ppermute(edges, "rad", [(0, 1), (1, 0)])
    else:
        inner = lax.ppermute(edges, "rad", [(i, i + 1) for i in range(rad_size - 1)])
        outer = lax.ppermute(edges, "rad", [(i + 1, i) for i in range(rad_size - 1)])
    wake_recv = [fetch(wk, s) for s in range(1, groups)]

    field_shape = (fields, rows, lanes)
    angle_shape = (steps, count, cols)
    angle = jax.ShapeDtypeStruct(angle_shape, f32)
    field = jax.ShapeDtypeStruct(field_shape, f32)
    plane = jax.ShapeDtypeStruct((rows, lanes), f32)
    own_flops = 2 * 2 * 3 * count * modes * steps * cols

    a_own, c_own = call(
        functools.partial(own_kernel, dims), steps, where,
        (adj, st, wake_coupling, own_table),
        [whole(field_shape), whole(field_shape), SMEM, chosen(own_table.shape)],
        [angle, angle],
        [stepped(angle_shape), stepped(angle_shape)],
        [pltpu.VMEM((3 * modes, cols), jnp.bfloat16)] * 2,
        own_flops,
    )

    chunk = 16 if modes % 32 == 0 else 8
    base = call(
        functools.partial(
            base_kernel, fields, modes, cells_ax, chunk, count, lanes * rad_size, rad_size
        ),
        1, where,
        (adj, below, above, inner, outer, jac_axial, jac_radial, jac_swirl),
        [whole(field_shape), whole(below.shape), whole(above.shape)]
        + [whole(edges.shape)] * 2 + [SMEM] * 3,
        [field], [whole(field_shape)], [],
        32 * fields * fields * rows * lanes,
    )[0]

    joined = call(
        functools.partial(join_kernel, dims, groups), steps, where,
        (*adj_recv, a_own, c_own, other_table, base),
        [whole(field_shape)] * (groups - 1)
        + [stepped(angle_shape), stepped(angle_shape), chosen(other_table.shape), ANY],
        [angle] + [plane] * groups,
        [stepped(angle_shape)] + [whole((rows, lanes))] * groups,
        [pltpu.VMEM((3 * modes, cols), jnp.bfloat16)],
        (groups - 1) * own_flops // 2,
    )
    a_all, parts = joined[0], joined[1:]
    part_recv = [deliver(parts[s], s) for s in range(1, groups)]

    adjoint_in = call(
        functools.partial(back_kernel, dims, groups), steps, where,
        (wk, *wake_recv, a_all, base, wake_coupling, back_table),
        [whole((rows, lanes))] * groups
        + [stepped(angle_shape), whole(field_shape), SMEM, chosen(back_table.shape)],
        [field], [whole(field_shape)],
        [pltpu.VMEM((3 * count, cols), jnp.bfloat16)],
        own_flops // 2,
    )[0]

    total = parts[0]
    for part in part_recv:
        total = total + part
    return (
        adjoint_in.reshape(adjoint.shape),
        (-total).reshape(wake.shape),
    )


def solution(mesh):
    return jax.shard_map(
        body,
        mesh=mesh,
        in_specs=(
            P(None, "mode", "ax", "rad"),
            P(None, "mode", "ax", "rad"),
            P("mode", "ax", "rad"),
            P(),
            P(),
            P(),
            P(),
        ),
        out_specs=(P(None, "mode", "ax", "rad"), P("mode", "ax", "rad")),
        check_vma=False,
    )
```

```python
import functools
import math

import jax
import jax.numpy as jnp
import ml_dtypes
import numpy as np
from jax import lax
from jax.experimental import pallas as pl
from jax.experimental.pallas import tpu as pltpu
from jax.sharding import PartitionSpec as P

VMEM_LIMIT = 32 * 1024 * 1024


def fourier_basis(count):
    angle = np.arange(count)[:, None]
    coef = np.arange(count)[None, :]
    phase = ((coef // 2) * angle % count) * (2.0 * math.pi / count)
    table = math.sqrt(2.0 / count) * np.where(coef % 2 == 0, np.cos(phase), np.sin(phase))
    table = np.where(coef == 0, 1.0 / math.sqrt(count), table)
    table = np.where(coef == 1, np.where(angle % 2 == 0, 1.0, -1.0) / math.sqrt(count), table)
    return table.astype(np.float32)


def three_terms(table):
    high = table.astype(ml_dtypes.bfloat16)
    low = (table - high.astype(np.float32)).astype(ml_dtypes.bfloat16)
    return np.concatenate([high, low, high], axis=-1)


def tables(groups, modes_here):
    count = groups * modes_here
    basis = fourier_basis(count)
    own, other, back = [], [], []
    for m in range(groups):
        rolled = np.roll(np.roll(basis, -m * modes_here, axis=0), -m * modes_here, axis=1)
        blocks = [rolled[:, s * modes_here : (s + 1) * modes_here] for s in range(groups)]
        own.append(three_terms(blocks[0]))
        other.append(np.stack([three_terms(block) for block in blocks[1:]]))
        back.append(three_terms(np.ascontiguousarray(blocks[0].T)))
    return np.stack(own), np.stack(other), np.stack(back)


def split(value):
    high = value.astype(jnp.bfloat16)
    low = (value - high.astype(jnp.float32)).astype(jnp.bfloat16)
    return high, low


def put_split(terms, row, rows, total, cols, value):
    high, low = split(value)
    terms[pl.ds(row, rows), cols] = high
    terms[pl.ds(total + row, rows), cols] = high
    terms[pl.ds(2 * total + row, rows), cols] = low


def pack_kernel(fields, modes, cells_ax, adj, first, last, edges):
    lanes = adj.shape[2]
    pair = lax.broadcasted_iota(jnp.int32, (modes, lanes), 1) // 2
    packed = jnp.zeros((modes, lanes), jnp.float32)
    for f in range(fields):
        for x in range(cells_ax):
            block = adj[f, pl.ds(x, modes, stride=cells_ax), :]
            if x == 0:
                first[f] = block
            if x == cells_ax - 1:
                last[f] = block
            j = f * cells_ax + x
            packed = jnp.where(pair == j, pltpu.roll(block, 2 * j + 1, 1), packed)
    edges[...] = packed


def own_kernel(dims, where, adj, state, coupling, table, a_out, c_out, terms_a, terms_c):
    fields, modes, cells_ax, width, cols_of = dims
    for j in range(width):
        x = pl.program_id(0) * width + j
        rows = pl.ds(x, modes, stride=cells_ax)
        for f in range(fields):
            put_split(terms_a, 0, modes, modes, cols_of(j, f), adj[f, rows, :])
    a_out[0] = jnp.dot(table[0], terms_a[...], preferred_element_type=jnp.float32)
    for j in range(width):
        x = pl.program_id(0) * width + j
        rows = pl.ds(x, modes, stride=cells_ax)
        for f in range(fields):
            mixed = coupling[f, 0] * state[0, rows, :]
            for e in range(1, fields):
                mixed = mixed + coupling[f, e] * state[e, rows, :]
            put_split(terms_c, 0, modes, modes, cols_of(j, f), mixed)
    c_out[0] = jnp.dot(table[0], terms_c[...], preferred_element_type=jnp.float32)


def join_kernel(dims, groups, cuts, where, *refs):
    fields, modes, cells_ax, width, cols_of = dims
    pieces = len(cuts) - 1
    recv = refs[: groups - 1]
    a_own, c_own, table, _, a_out = refs[groups - 1 : groups + 4]
    h_out = refs[groups + 4 : -1]
    terms = refs[-1]
    total = a_own[0]
    for s in range(groups - 1):
        for j in range(width):
            x = pl.program_id(0) * width + j
            rows = pl.ds(x, modes, stride=cells_ax)
            for f in range(fields):
                put_split(terms, 0, modes, modes, cols_of(j, f), recv[s][f, rows, :])
        total = total + jnp.dot(table[0, s], terms[...], preferred_element_type=jnp.float32)
    a_out[0] = total
    for j in range(width):
        x = pl.program_id(0) * width + j
        for s, k in ((s, k) for s in range(groups) for k in range(pieces)):
            here = pl.ds(s * modes + cuts[k], cuts[k + 1] - cuts[k])
            rows = pl.ds(x, cuts[k + 1] - cuts[k], stride=cells_ax)
            part = a_out[0, here, cols_of(j, 0)] * c_own[0, here, cols_of(j, 0)]
            for f in range(1, fields):
                part = part + a_out[0, here, cols_of(j, f)] * c_own[0, here, cols_of(j, f)]
            h_out[s * pieces + k][rows, :] = part


def total_kernel(terms, *refs):
    total = refs[0][...]
    for ref in refs[1:terms]:
        total = total + ref[...]
    refs[-1][...] = -total


def back_kernel(dims, groups, where, *refs):
    fields, modes, cells_ax, width, cols_of = dims
    wakes = refs[:groups]
    angle, base, coupling, table, out, terms = refs[groups:]
    count = groups * modes
    for j in range(width):
        x = pl.program_id(0) * width + j
        rows = pl.ds(x, modes, stride=cells_ax)
        for s in range(groups):
            wake = wakes[s][rows, :]
            for f in range(fields):
                scaled = wake * angle[0, pl.ds(s * modes, modes), cols_of(j, f)]
                put_split(terms, s * modes, modes, count, cols_of(j, f), scaled)
    returned = jnp.dot(table[0], terms[...], preferred_element_type=jnp.float32)
    for j in range(width):
        x = pl.program_id(0) * width + j
        rows = pl.ds(x, modes, stride=cells_ax)
        for f in range(fields):
            value = base[f, rows, :]
            for e in range(fields):
                value = value - coupling[e, f] * returned[:, cols_of(j, e)]
            out[f, rows, :] = value


def base_kernel(
    fields, modes, cells_ax, chunk, mode_total, rad_total, rad_size,
    where, adj, below, above, inner, outer, jac_axial, jac_radial, jac_swirl, out,
):
    lanes = adj.shape[2]
    half = modes // 2
    rad = where[1]
    lane = lax.broadcasted_iota(jnp.int32, (chunk, lanes), 1)
    row = lax.broadcasted_iota(jnp.int32, (chunk, lanes), 0)
    radius = 0.5 + ((rad * lanes + lane).astype(jnp.float32) + 0.5) / jnp.float32(2.0 * rad_total)
    swirl = 0.25 / radius
    has_inner = jnp.where((lane == 0) & (rad == 0), 0.0, 0.5)
    has_outer = jnp.where((lane == lanes - 1) & (rad == rad_size - 1), 0.0, 0.5)

    def step(i, carry):
        order = (where[0] * half + i * chunk + row).astype(jnp.float32) / jnp.float32(mode_total // 2)
        rate = swirl * order
        for p in range(2):
            halo = pl.ds(2 * i * chunk + p, chunk, stride=2)
            edges = jnp.where(lane % 2 == 0, pltpu.roll(inner[halo, :], 2, 1), outer[halo, :])
            for x in range(cells_ax):
                def at(e, parity, cell):
                    start = (2 * i * chunk + parity) * cells_ax + cell
                    return adj[e, pl.ds(start, chunk, stride=2 * cells_ax), :]

                here = pl.ds((2 * i * chunk + p) * cells_ax + x, chunk, stride=2 * cells_ax)
                total = [None] * fields
                for e in range(fields):
                    centre = at(e, p, x)
                    low = below[e, halo, :] if x == 0 else at(e, p, x - 1)
                    high = above[e, halo, :] if x == cells_ax - 1 else at(e, p, x + 1)
                    axial = 0.5 * (high - low)
                    edge = pltpu.roll(edges, lanes - 2 * (e * cells_ax + x) - 2, 1)
                    inward = jnp.where(lane == 0, edge, pltpu.roll(centre, 1, 1))
                    outward = jnp.where(lane == lanes - 1, edge, pltpu.roll(centre, lanes - 1, 1))
                    radial = has_outer * outward - has_inner * inward
                    turned = (rate if p == 0 else -rate) * at(e, 1 - p, x)
                    for f in range(fields):
                        term = (
                            jac_axial[e, f] * axial
                            + jac_radial[e, f] * radial
                            + jac_swirl[e, f] * turned
                        )
                        if f == e:
                            term = term + centre
                        total[f] = term if e == 0 else total[f] + term
                for f in range(fields):
                    out[f, here, :] = total[f]
        return carry

    lax.fori_loop(0, half // chunk, step, 0)


def whole(shape):
    return pl.BlockSpec(shape, lambda i, where: (0,) * len(shape))


def stepped(shape):
    return pl.BlockSpec((1, *shape[1:]), lambda i, where: (i,) + (0,) * (len(shape) - 1))


def chosen(shape):
    return pl.BlockSpec((1, *shape[1:]), lambda i, where: (where[0],) + (0,) * (len(shape) - 1))


SMEM = pl.BlockSpec(memory_space=pltpu.SMEM)
ANY = pl.BlockSpec(memory_space=pl.ANY)


def call(kernel, steps, where, args, in_specs, outs, out_specs, scratch, flops):
    moved = sum(a.size * a.dtype.itemsize for a in args) + sum(o.size * o.dtype.itemsize for o in outs)
    return pl.pallas_call(
        kernel,
        grid_spec=pltpu.PrefetchScalarGridSpec(
            num_scalar_prefetch=1,
            grid=(steps,),
            in_specs=in_specs,
            out_specs=out_specs,
            scratch_shapes=scratch,
        ),
        out_shape=outs,
        compiler_params=pltpu.CompilerParams(vmem_limit_bytes=VMEM_LIMIT),
        cost_estimate=pl.CostEstimate(flops=flops, bytes_accessed=moved, transcendentals=0),
    )(where, *args)


def body(adjoint, state, wake, jac_axial, jac_radial, jac_swirl, wake_coupling):
    fields, modes, cells_ax, lanes = adjoint.shape
    groups = lax.axis_size("mode")
    count = groups * modes
    rad_size = lax.axis_size("rad")
    ax_size = lax.axis_size("ax")
    width = 2 if cells_ax % 2 == 0 else 1
    steps = cells_ax // width
    rows = modes * cells_ax
    cols = width * fields * lanes
    f32 = jnp.float32

    def cols_of(j, f):
        return pl.ds((j * fields + f) * lanes, lanes)

    dims = (fields, modes, cells_ax, width, cols_of)
    own_table, other_table, back_table = tables(groups, modes)
    where = jnp.stack([lax.axis_index("mode"), lax.axis_index("rad")]).astype(jnp.int32)

    adj = adjoint.reshape(fields, rows, lanes)
    st = state.reshape(fields, rows, lanes)
    wk = wake.reshape(rows, lanes)

    def fetch(value, s):
        return lax.ppermute(value, "mode", [((i + s) % groups, i) for i in range(groups)])

    def deliver(value, s):
        return lax.ppermute(value, "mode", [(i, (i + s) % groups) for i in range(groups)])

    adj_recv = [fetch(adj, s) for s in range(1, groups)]

    up = [(i, i + 1) for i in range(ax_size - 1)]
    down = [(i + 1, i) for i in range(ax_size - 1)]
    layer = jax.ShapeDtypeStruct((fields, modes, lanes), adjoint.dtype)
    first, last, edges = pl.pallas_call(
        functools.partial(pack_kernel, fields, modes, cells_ax),
        out_shape=[layer, layer, jax.ShapeDtypeStruct((modes, lanes), adjoint.dtype)],
        compiler_params=pltpu.CompilerParams(vmem_limit_bytes=VMEM_LIMIT),
    )(adj)
    below = lax.ppermute(last, "ax", up)
    above = lax.ppermute(first, "ax", down)
    if rad_size == 2:
        inner = outer = lax.ppermute(edges, "rad", [(0, 1), (1, 0)])
    else:
        inner = lax.ppermute(edges, "rad", [(i, i + 1) for i in range(rad_size - 1)])
        outer = lax.ppermute(edges, "rad", [(i + 1, i) for i in range(rad_size - 1)])
    wake_recv = [fetch(wk, s) for s in range(1, groups)]

    field_shape = (fields, rows, lanes)
    angle_shape = (steps, count, cols)
    angle = jax.ShapeDtypeStruct(angle_shape, f32)
    field = jax.ShapeDtypeStruct(field_shape, f32)
    plane = jax.ShapeDtypeStruct((rows, lanes), f32)
    own_flops = 2 * 2 * 3 * count * modes * steps * cols

    a_own, c_own = call(
        functools.partial(own_kernel, dims), steps, where,
        (adj, st, wake_coupling, own_table),
        [whole(field_shape), whole(field_shape), SMEM, chosen(own_table.shape)],
        [angle, angle],
        [stepped(angle_shape), stepped(angle_shape)],
        [pltpu.VMEM((3 * modes, cols), jnp.bfloat16)] * 2,
        own_flops,
    )

    chunk = 16 if modes % 32 == 0 else 8
    base = call(
        functools.partial(
            base_kernel, fields, modes, cells_ax, chunk, count, lanes * rad_size, rad_size
        ),
        1, where,
        (adj, below, above, inner, outer, jac_axial, jac_radial, jac_swirl),
        [whole(field_shape), whole(below.shape), whole(above.shape)]
        + [whole(edges.shape)] * 2 + [SMEM] * 3,
        [field], [whole(field_shape)], [],
        32 * fields * fields * rows * lanes,
    )[0]

    cuts = (0, modes // 2, modes)
    pieces = len(cuts) - 1
    piece_rows = [(cuts[k + 1] - cuts[k]) * cells_ax for k in range(pieces)]
    joined = call(
        functools.partial(join_kernel, dims, groups, cuts), steps, where,
        (*adj_recv, a_own, c_own, other_table, base),
        [whole(field_shape)] * (groups - 1)
        + [stepped(angle_shape), stepped(angle_shape), chosen(other_table.shape), ANY],
        [angle] + [jax.ShapeDtypeStruct((n, lanes), f32) for n in piece_rows] * groups,
        [stepped(angle_shape)] + [whole((n, lanes)) for n in piece_rows] * groups,
        [pltpu.VMEM((3 * modes, cols), jnp.bfloat16)],
        (groups - 1) * own_flops // 2,
    )
    a_all = joined[0]
    parts = [joined[1 + k :: pieces] for k in range(pieces)]
    arrived = [[deliver(part[s], s) for s in range(1, groups)] for part in parts]

    adjoint_in = call(
        functools.partial(back_kernel, dims, groups), steps, where,
        (wk, *wake_recv, a_all, base, wake_coupling, back_table),
        [whole((rows, lanes))] * groups
        + [stepped(angle_shape), whole(field_shape), SMEM, chosen(back_table.shape)],
        [field], [whole(field_shape)],
        [pltpu.VMEM((3 * count, cols), jnp.bfloat16)],
        own_flops // 2,
    )[0]

    wake_grad = None
    for k in range(pieces):
        size, place = piece_rows[k], cuts[k] * cells_ax
        wake_grad = pl.pallas_call(
            functools.partial(total_kernel, groups),
            grid=(1,),
            out_shape=plane,
            in_specs=[pl.BlockSpec((size, lanes), lambda i: (0, 0))] * groups
            + ([] if wake_grad is None else [ANY]),
            out_specs=pl.BlockSpec((size, lanes), lambda i, at=place // size: (at, 0)),
            input_output_aliases={} if wake_grad is None else {groups: 0},
            compiler_params=pltpu.CompilerParams(vmem_limit_bytes=VMEM_LIMIT),
        )(parts[k][0], *arrived[k], *([] if wake_grad is None else [wake_grad]))
    return (
        adjoint_in.reshape(adjoint.shape),
        wake_grad.reshape(wake.shape),
    )


def solution(mesh):
    return jax.shard_map(
        body,
        mesh=mesh,
        in_specs=(
            P(None, "mode", "ax", "rad"),
            P(None, "mode", "ax", "rad"),
            P("mode", "ax", "rad"),
            P(),
            P(),
            P(),
            P(),
        ),
        out_specs=(P(None, "mode", "ax", "rad"), P("mode", "ax", "rad")),
        check_vma=False,
    )
```

```python
import functools
import math

import jax
import jax.numpy as jnp
import ml_dtypes
import numpy as np
from jax import lax
from jax.experimental import pallas as pl
from jax.experimental.pallas import tpu as pltpu
from jax.sharding import PartitionSpec as P

VMEM_LIMIT = 32 * 1024 * 1024


def fourier_basis(count):
    angle = np.arange(count)[:, None]
    coef = np.arange(count)[None, :]
    phase = ((coef // 2) * angle % count) * (2.0 * math.pi / count)
    table = math.sqrt(2.0 / count) * np.where(coef % 2 == 0, np.cos(phase), np.sin(phase))
    table = np.where(coef == 0, 1.0 / math.sqrt(count), table)
    table = np.where(coef == 1, np.where(angle % 2 == 0, 1.0, -1.0) / math.sqrt(count), table)
    return table.astype(np.float32)


def three_terms(table):
    high = table.astype(ml_dtypes.bfloat16)
    low = (table - high.astype(np.float32)).astype(ml_dtypes.bfloat16)
    return np.concatenate([high, low, high], axis=-1)


def tables(groups, modes_here):
    count = groups * modes_here
    basis = fourier_basis(count)
    own, other, back = [], [], []
    for m in range(groups):
        rolled = np.roll(np.roll(basis, -m * modes_here, axis=0), -m * modes_here, axis=1)
        blocks = [rolled[:, s * modes_here : (s + 1) * modes_here] for s in range(groups)]
        own.append(three_terms(blocks[0]))
        other.append(np.stack([three_terms(block) for block in blocks[1:]]))
        back.append(three_terms(np.ascontiguousarray(blocks[0].T)))
    return np.stack(own), np.stack(other), np.stack(back)


def split(value):
    high = value.astype(jnp.bfloat16)
    low = (value - high.astype(jnp.float32)).astype(jnp.bfloat16)
    return high, low


def put_split(terms, row, rows, total, cols, value):
    high, low = split(value)
    terms[pl.ds(row, rows), cols] = high
    terms[pl.ds(total + row, rows), cols] = high
    terms[pl.ds(2 * total + row, rows), cols] = low


def pack_kernel(fields, modes, cells_ax, adj, first, last, edges):
    lanes = adj.shape[2]
    pair = lax.broadcasted_iota(jnp.int32, (modes, lanes), 1) // 2
    packed = jnp.zeros((modes, lanes), jnp.float32)
    for f in range(fields):
        for x in range(cells_ax):
            block = adj[f, pl.ds(x, modes, stride=cells_ax), :]
            if x == 0:
                first[f] = block
            if x == cells_ax - 1:
                last[f] = block
            j = f * cells_ax + x
            packed = jnp.where(pair == j, pltpu.roll(block, 2 * j + 1, 1), packed)
    edges[...] = packed


def own_kernel(dims, where, adj, state, coupling, table, a_out, c_out, terms_a, terms_c):
    fields, modes, cells_ax, width, cols_of = dims
    for j in range(width):
        x = pl.program_id(0) * width + j
        rows = pl.ds(x, modes, stride=cells_ax)
        for f in range(fields):
            put_split(terms_a, 0, modes, modes, cols_of(j, f), adj[f, rows, :])
    a_out[0] = jnp.dot(table[0], terms_a[...], preferred_element_type=jnp.float32)
    for j in range(width):
        x = pl.program_id(0) * width + j
        rows = pl.ds(x, modes, stride=cells_ax)
        for f in range(fields):
            mixed = coupling[f, 0] * state[0, rows, :]
            for e in range(1, fields):
                mixed = mixed + coupling[f, e] * state[e, rows, :]
            put_split(terms_c, 0, modes, modes, cols_of(j, f), mixed)
    c_out[0] = jnp.dot(table[0], terms_c[...], preferred_element_type=jnp.float32)


def join_kernel(dims, groups, cuts, where, *refs):
    fields, modes, cells_ax, width, cols_of = dims
    pieces = len(cuts) - 1
    recv = refs[: groups - 1]
    a_own, c_own, table, _, a_out = refs[groups - 1 : groups + 4]
    h_out = refs[groups + 4 : -1]
    terms = refs[-1]
    total = a_own[0]
    for s in range(groups - 1):
        for j in range(width):
            x = pl.program_id(0) * width + j
            rows = pl.ds(x, modes, stride=cells_ax)
            for f in range(fields):
                put_split(terms, 0, modes, modes, cols_of(j, f), recv[s][f, rows, :])
        total = total + jnp.dot(table[0, s], terms[...], preferred_element_type=jnp.float32)
    a_out[0] = total
    for j in range(width):
        x = pl.program_id(0) * width + j
        for s, k in ((s, k) for s in range(groups) for k in range(pieces)):
            here = pl.ds(s * modes + cuts[k], cuts[k + 1] - cuts[k])
            rows = pl.ds(x, cuts[k + 1] - cuts[k], stride=cells_ax)
            part = a_out[0, here, cols_of(j, 0)] * c_own[0, here, cols_of(j, 0)]
            for f in range(1, fields):
                part = part + a_out[0, here, cols_of(j, f)] * c_own[0, here, cols_of(j, f)]
            h_out[s * pieces + k][rows, :] = part


def sum_kernel(*refs):
    total = refs[0][...]
    for ref in refs[1:-1]:
        total = total + ref[...]
    refs[-1][...] = total


def total_kernel(cut, *refs):
    out = refs[-1]
    out[pl.ds(0, cut), :] = -refs[0][...]
    total = refs[1][...]
    for ref in refs[2:-1]:
        total = total + ref[...]
    out[pl.ds(cut, out.shape[0] - cut), :] = -total


def back_kernel(dims, groups, where, *refs):
    fields, modes, cells_ax, width, cols_of = dims
    wakes = refs[:groups]
    angle, base, coupling, table, out, terms = refs[groups:]
    count = groups * modes
    for j in range(width):
        x = pl.program_id(0) * width + j
        rows = pl.ds(x, modes, stride=cells_ax)
        for s in range(groups):
            wake = wakes[s][rows, :]
            for f in range(fields):
                scaled = wake * angle[0, pl.ds(s * modes, modes), cols_of(j, f)]
                put_split(terms, s * modes, modes, count, cols_of(j, f), scaled)
    returned = jnp.dot(table[0], terms[...], preferred_element_type=jnp.float32)
    for j in range(width):
        x = pl.program_id(0) * width + j
        rows = pl.ds(x, modes, stride=cells_ax)
        for f in range(fields):
            value = base[f, rows, :]
            for e in range(fields):
                value = value - coupling[e, f] * returned[:, cols_of(j, e)]
            out[f, rows, :] = value


def base_kernel(
    fields, modes, cells_ax, chunk, mode_total, rad_total, rad_size,
    where, adj, below, above, inner, outer, jac_axial, jac_radial, jac_swirl, out,
):
    lanes = adj.shape[2]
    half = modes // 2
    rad = where[1]
    lane = lax.broadcasted_iota(jnp.int32, (chunk, lanes), 1)
    row = lax.broadcasted_iota(jnp.int32, (chunk, lanes), 0)
    radius = 0.5 + ((rad * lanes + lane).astype(jnp.float32) + 0.5) / jnp.float32(2.0 * rad_total)
    swirl = 0.25 / radius
    has_inner = jnp.where((lane == 0) & (rad == 0), 0.0, 0.5)
    has_outer = jnp.where((lane == lanes - 1) & (rad == rad_size - 1), 0.0, 0.5)

    def step(i, carry):
        order = (where[0] * half + i * chunk + row).astype(jnp.float32) / jnp.float32(mode_total // 2)
        rate = swirl * order
        for p in range(2):
            halo = pl.ds(2 * i * chunk + p, chunk, stride=2)
            edges = jnp.where(lane % 2 == 0, pltpu.roll(inner[halo, :], 2, 1), outer[halo, :])
            for x in range(cells_ax):
                def at(e, parity, cell):
                    start = (2 * i * chunk + parity) * cells_ax + cell
                    return adj[e, pl.ds(start, chunk, stride=2 * cells_ax), :]

                here = pl.ds((2 * i * chunk + p) * cells_ax + x, chunk, stride=2 * cells_ax)
                total = [None] * fields
                for e in range(fields):
                    centre = at(e, p, x)
                    low = below[e, halo, :] if x == 0 else at(e, p, x - 1)
                    high = above[e, halo, :] if x == cells_ax - 1 else at(e, p, x + 1)
                    axial = 0.5 * (high - low)
                    edge = pltpu.roll(edges, lanes - 2 * (e * cells_ax + x) - 2, 1)
                    inward = jnp.where(lane == 0, edge, pltpu.roll(centre, 1, 1))
                    outward = jnp.where(lane == lanes - 1, edge, pltpu.roll(centre, lanes - 1, 1))
                    radial = has_outer * outward - has_inner * inward
                    turned = (rate if p == 0 else -rate) * at(e, 1 - p, x)
                    for f in range(fields):
                        term = (
                            jac_axial[e, f] * axial
                            + jac_radial[e, f] * radial
                            + jac_swirl[e, f] * turned
                        )
                        if f == e:
                            term = term + centre
                        total[f] = term if e == 0 else total[f] + term
                for f in range(fields):
                    out[f, here, :] = total[f]
        return carry

    lax.fori_loop(0, half // chunk, step, 0)


def whole(shape):
    return pl.BlockSpec(shape, lambda i, where: (0,) * len(shape))


def stepped(shape):
    return pl.BlockSpec((1, *shape[1:]), lambda i, where: (i,) + (0,) * (len(shape) - 1))


def chosen(shape):
    return pl.BlockSpec((1, *shape[1:]), lambda i, where: (where[0],) + (0,) * (len(shape) - 1))


SMEM = pl.BlockSpec(memory_space=pltpu.SMEM)
ANY = pl.BlockSpec(memory_space=pl.ANY)


def call(kernel, steps, where, args, in_specs, outs, out_specs, scratch, flops):
    moved = sum(a.size * a.dtype.itemsize for a in args) + sum(o.size * o.dtype.itemsize for o in outs)
    return pl.pallas_call(
        kernel,
        grid_spec=pltpu.PrefetchScalarGridSpec(
            num_scalar_prefetch=1,
            grid=(steps,),
            in_specs=in_specs,
            out_specs=out_specs,
            scratch_shapes=scratch,
        ),
        out_shape=outs,
        compiler_params=pltpu.CompilerParams(vmem_limit_bytes=VMEM_LIMIT),
        cost_estimate=pl.CostEstimate(flops=flops, bytes_accessed=moved, transcendentals=0),
    )(where, *args)


def body(adjoint, state, wake, jac_axial, jac_radial, jac_swirl, wake_coupling):
    fields, modes, cells_ax, lanes = adjoint.shape
    groups = lax.axis_size("mode")
    count = groups * modes
    rad_size = lax.axis_size("rad")
    ax_size = lax.axis_size("ax")
    width = 2 if cells_ax % 2 == 0 else 1
    steps = cells_ax // width
    rows = modes * cells_ax
    cols = width * fields * lanes
    f32 = jnp.float32

    def cols_of(j, f):
        return pl.ds((j * fields + f) * lanes, lanes)

    dims = (fields, modes, cells_ax, width, cols_of)
    own_table, other_table, back_table = tables(groups, modes)
    where = jnp.stack([lax.axis_index("mode"), lax.axis_index("rad")]).astype(jnp.int32)

    adj = adjoint.reshape(fields, rows, lanes)
    st = state.reshape(fields, rows, lanes)
    wk = wake.reshape(rows, lanes)

    def fetch(value, s):
        return lax.ppermute(value, "mode", [((i + s) % groups, i) for i in range(groups)])

    def deliver(value, s):
        return lax.ppermute(value, "mode", [(i, (i + s) % groups) for i in range(groups)])

    adj_recv = [fetch(adj, s) for s in range(1, groups)]

    up = [(i, i + 1) for i in range(ax_size - 1)]
    down = [(i + 1, i) for i in range(ax_size - 1)]
    layer = jax.ShapeDtypeStruct((fields, modes, lanes), adjoint.dtype)
    first, last, edges = pl.pallas_call(
        functools.partial(pack_kernel, fields, modes, cells_ax),
        out_shape=[layer, layer, jax.ShapeDtypeStruct((modes, lanes), adjoint.dtype)],
        compiler_params=pltpu.CompilerParams(vmem_limit_bytes=VMEM_LIMIT),
    )(adj)
    below = lax.ppermute(last, "ax", up)
    above = lax.ppermute(first, "ax", down)
    if rad_size == 2:
        inner = outer = lax.ppermute(edges, "rad", [(0, 1), (1, 0)])
    else:
        inner = lax.ppermute(edges, "rad", [(i, i + 1) for i in range(rad_size - 1)])
        outer = lax.ppermute(edges, "rad", [(i + 1, i) for i in range(rad_size - 1)])
    wake_recv = [fetch(wk, s) for s in range(1, groups)]

    field_shape = (fields, rows, lanes)
    angle_shape = (steps, count, cols)
    angle = jax.ShapeDtypeStruct(angle_shape, f32)
    field = jax.ShapeDtypeStruct(field_shape, f32)
    plane = jax.ShapeDtypeStruct((rows, lanes), f32)
    own_flops = 2 * 2 * 3 * count * modes * steps * cols

    a_own, c_own = call(
        functools.partial(own_kernel, dims), steps, where,
        (adj, st, wake_coupling, own_table),
        [whole(field_shape), whole(field_shape), SMEM, chosen(own_table.shape)],
        [angle, angle],
        [stepped(angle_shape), stepped(angle_shape)],
        [pltpu.VMEM((3 * modes, cols), jnp.bfloat16)] * 2,
        own_flops,
    )

    chunk = 16 if modes % 32 == 0 else 8
    base = call(
        functools.partial(
            base_kernel, fields, modes, cells_ax, chunk, count, lanes * rad_size, rad_size
        ),
        1, where,
        (adj, below, above, inner, outer, jac_axial, jac_radial, jac_swirl),
        [whole(field_shape), whole(below.shape), whole(above.shape)]
        + [whole(edges.shape)] * 2 + [SMEM] * 3,
        [field], [whole(field_shape)], [],
        32 * fields * fields * rows * lanes,
    )[0]

    cuts = (0, modes * 3 // 4 // 8 * 8, modes)
    pieces = len(cuts) - 1
    piece_rows = [(cuts[k + 1] - cuts[k]) * cells_ax for k in range(pieces)]
    joined = call(
        functools.partial(join_kernel, dims, groups, cuts), steps, where,
        (*adj_recv, a_own, c_own, other_table, base),
        [whole(field_shape)] * (groups - 1)
        + [stepped(angle_shape), stepped(angle_shape), chosen(other_table.shape), ANY],
        [angle] + [jax.ShapeDtypeStruct((n, lanes), f32) for n in piece_rows] * groups,
        [stepped(angle_shape)] + [whole((n, lanes)) for n in piece_rows] * groups,
        [pltpu.VMEM((3 * modes, cols), jnp.bfloat16)],
        (groups - 1) * own_flops // 2,
    )
    a_all = joined[0]
    parts = [joined[1 + k :: pieces] for k in range(pieces)]
    arrived = [[deliver(part[s], s) for s in range(1, groups)] for part in parts[:1]]
    if groups == 2 and rad_size == 2:
        sibling = lax.ppermute(parts[1][1], "rad", [(0, 1), (1, 0)])
        arrived.append([lax.ppermute(sibling, ("mode", "rad"), [(i, 3 - i) for i in range(4)])])
    else:
        arrived.append([deliver(parts[1][s], s) for s in range(1, groups)])

    adjoint_in = call(
        functools.partial(back_kernel, dims, groups), steps, where,
        (wk, *wake_recv, a_all, base, wake_coupling, back_table),
        [whole((rows, lanes))] * groups
        + [stepped(angle_shape), whole(field_shape), SMEM, chosen(back_table.shape)],
        [field], [whole(field_shape)],
        [pltpu.VMEM((3 * count, cols), jnp.bfloat16)],
        own_flops // 2,
    )[0]

    early = pl.pallas_call(
        sum_kernel,
        out_shape=jax.ShapeDtypeStruct(parts[0][0].shape, f32),
        compiler_params=pltpu.CompilerParams(vmem_limit_bytes=VMEM_LIMIT),
    )(parts[0][0], *arrived[0])
    wake_grad = pl.pallas_call(
        functools.partial(total_kernel, piece_rows[0]),
        out_shape=plane,
        compiler_params=pltpu.CompilerParams(vmem_limit_bytes=VMEM_LIMIT),
    )(early, parts[1][0], *arrived[1])
    return (
        adjoint_in.reshape(adjoint.shape),
        wake_grad.reshape(wake.shape),
    )


def solution(mesh):
    return jax.shard_map(
        body,
        mesh=mesh,
        in_specs=(
            P(None, "mode", "ax", "rad"),
            P(None, "mode", "ax", "rad"),
            P("mode", "ax", "rad"),
            P(),
            P(),
            P(),
            P(),
        ),
        out_specs=(P(None, "mode", "ax", "rad"), P("mode", "ax", "rad")),
        check_vma=False,
    )
```

```python
import functools
import math

import jax
import jax.numpy as jnp
import ml_dtypes
import numpy as np
from jax import lax
from jax.experimental import pallas as pl
from jax.experimental.pallas import tpu as pltpu
from jax.sharding import PartitionSpec as P

VMEM_LIMIT = 32 * 1024 * 1024


def fourier_basis(count):
    angle = np.arange(count)[:, None]
    coef = np.arange(count)[None, :]
    phase = ((coef // 2) * angle % count) * (2.0 * math.pi / count)
    table = math.sqrt(2.0 / count) * np.where(coef % 2 == 0, np.cos(phase), np.sin(phase))
    table = np.where(coef == 0, 1.0 / math.sqrt(count), table)
    table = np.where(coef == 1, np.where(angle % 2 == 0, 1.0, -1.0) / math.sqrt(count), table)
    return table.astype(np.float32)


def three_terms(table):
    high = table.astype(ml_dtypes.bfloat16)
    low = (table - high.astype(np.float32)).astype(ml_dtypes.bfloat16)
    return np.concatenate([high, low, high], axis=-1)


def two_terms(table):
    high = table.astype(ml_dtypes.bfloat16)
    low = (table - high.astype(np.float32)).astype(ml_dtypes.bfloat16)
    return np.concatenate([high, low], axis=0)


def tables(groups, modes_here):
    count = groups * modes_here
    basis = fourier_basis(count)
    own, other, back = [], [], []
    for m in range(groups):
        rolled = np.roll(np.roll(basis, -m * modes_here, axis=0), -m * modes_here, axis=1)
        blocks = [rolled[:, s * modes_here : (s + 1) * modes_here] for s in range(groups)]
        own.append(three_terms(blocks[0]))
        other.append(np.stack([three_terms(block) for block in blocks[1:]]))
        back.append(two_terms(np.ascontiguousarray(blocks[0].T)))
    return np.stack(own), np.stack(other), np.stack(back)


def split(value):
    high = value.astype(jnp.bfloat16)
    low = (value - high.astype(jnp.float32)).astype(jnp.bfloat16)
    return high, low


def put_split(terms, row, rows, total, cols, value):
    high, low = split(value)
    terms[pl.ds(row, rows), cols] = high
    terms[pl.ds(total + row, rows), cols] = high
    terms[pl.ds(2 * total + row, rows), cols] = low


def pack_kernel(fields, modes, cells_ax, adj, first, last, edges):
    lanes = adj.shape[2]
    pair = lax.broadcasted_iota(jnp.int32, (modes, lanes), 1) // 2
    packed = jnp.zeros((modes, lanes), jnp.float32)
    for f in range(fields):
        for x in range(cells_ax):
            block = adj[f, pl.ds(x, modes, stride=cells_ax), :]
            if x == 0:
                first[f] = block
            if x == cells_ax - 1:
                last[f] = block
            j = f * cells_ax + x
            packed = jnp.where(pair == j, pltpu.roll(block, 2 * j + 1, 1), packed)
    edges[...] = packed


def own_kernel(dims, where, adj, state, coupling, table, a_out, c_out, terms_a, terms_c):
    fields, modes, cells_ax, width, cols_of = dims
    for j in range(width):
        x = pl.program_id(0) * width + j
        rows = pl.ds(x, modes, stride=cells_ax)
        for f in range(fields):
            put_split(terms_a, 0, modes, modes, cols_of(j, f), adj[f, rows, :])
    a_out[0] = jnp.dot(table[0], terms_a[...], preferred_element_type=jnp.float32)
    for j in range(width):
        x = pl.program_id(0) * width + j
        rows = pl.ds(x, modes, stride=cells_ax)
        for f in range(fields):
            mixed = coupling[f, 0] * state[0, rows, :]
            for e in range(1, fields):
                mixed = mixed + coupling[f, e] * state[e, rows, :]
            put_split(terms_c, 0, modes, modes, cols_of(j, f), mixed)
    c_out[0] = jnp.dot(table[0], terms_c[...], preferred_element_type=jnp.float32)


def join_kernel(dims, groups, cuts, where, *refs):
    fields, modes, cells_ax, width, cols_of = dims
    pieces = len(cuts) - 1
    recv = refs[: groups - 1]
    a_own, c_own, table, _, a_out = refs[groups - 1 : groups + 4]
    h_out = refs[groups + 4 : -1]
    terms = refs[-1]
    total = a_own[0]
    for s in range(groups - 1):
        for j in range(width):
            x = pl.program_id(0) * width + j
            rows = pl.ds(x, modes, stride=cells_ax)
            for f in range(fields):
                put_split(terms, 0, modes, modes, cols_of(j, f), recv[s][f, rows, :])
        total = total + jnp.dot(table[0, s], terms[...], preferred_element_type=jnp.float32)
    a_out[0] = total
    for j in range(width):
        x = pl.program_id(0) * width + j
        for s, k in ((s, k) for s in range(groups) for k in range(pieces)):
            here = pl.ds(s * modes + cuts[k], cuts[k + 1] - cuts[k])
            rows = pl.ds(x, cuts[k + 1] - cuts[k], stride=cells_ax)
            part = a_out[0, here, cols_of(j, 0)] * c_own[0, here, cols_of(j, 0)]
            for f in range(1, fields):
                part = part + a_out[0, here, cols_of(j, f)] * c_own[0, here, cols_of(j, f)]
            h_out[s * pieces + k][rows, :] = part


def back_kernel(dims, groups, where, *refs):
    fields, modes, cells_ax, width, cols_of = dims
    wakes = refs[:groups]
    angle, base, coupling, table, out, terms = refs[groups:]
    count = groups * modes
    for j in range(width):
        x = pl.program_id(0) * width + j
        rows = pl.ds(x, modes, stride=cells_ax)
        for s in range(groups):
            wake = wakes[s][rows, :]
            for f in range(fields):
                scaled = wake * angle[0, pl.ds(s * modes, modes), cols_of(j, f)]
                high, low = split(scaled)
                terms[pl.ds(s * modes, modes), cols_of(j, f)] = high
                terms[pl.ds(count + s * modes, modes), cols_of(j, f)] = low
    both = jnp.dot(table[0], terms[pl.ds(0, count), :], preferred_element_type=jnp.float32)
    rest = jnp.dot(
        table[0, pl.ds(0, modes), :], terms[pl.ds(count, count), :], preferred_element_type=jnp.float32
    )
    returned = both[:modes] + (both[modes:] + rest)
    for j in range(width):
        x = pl.program_id(0) * width + j
        rows = pl.ds(x, modes, stride=cells_ax)
        for f in range(fields):
            value = base[f, rows, :]
            for e in range(fields):
                value = value - coupling[e, f] * returned[:, cols_of(j, e)]
            out[f, rows, :] = value


def base_kernel(
    fields, modes, cells_ax, chunk, mode_total, rad_total, rad_size,
    where, adj, below, above, inner, outer, jac_axial, jac_radial, jac_swirl, out,
):
    lanes = adj.shape[2]
    half = modes // 2
    rad = where[1]
    lane = lax.broadcasted_iota(jnp.int32, (chunk, lanes), 1)
    row = lax.broadcasted_iota(jnp.int32, (chunk, lanes), 0)
    radius = 0.5 + ((rad * lanes + lane).astype(jnp.float32) + 0.5) / jnp.float32(2.0 * rad_total)
    swirl = 0.25 / radius
    has_inner = jnp.where((lane == 0) & (rad == 0), 0.0, 0.5)
    has_outer = jnp.where((lane == lanes - 1) & (rad == rad_size - 1), 0.0, 0.5)

    def step(i, carry):
        order = (where[0] * half + i * chunk + row).astype(jnp.float32) / jnp.float32(mode_total // 2)
        rate = swirl * order
        for p in range(2):
            halo = pl.ds(2 * i * chunk + p, chunk, stride=2)
            edges = jnp.where(lane % 2 == 0, pltpu.roll(inner[halo, :], 2, 1), outer[halo, :])
            for x in range(cells_ax):
                def at(e, parity, cell):
                    start = (2 * i * chunk + parity) * cells_ax + cell
                    return adj[e, pl.ds(start, chunk, stride=2 * cells_ax), :]

                here = pl.ds((2 * i * chunk + p) * cells_ax + x, chunk, stride=2 * cells_ax)
                total = [None] * fields
                for e in range(fields):
                    centre = at(e, p, x)
                    low = below[e, halo, :] if x == 0 else at(e, p, x - 1)
                    high = above[e, halo, :] if x == cells_ax - 1 else at(e, p, x + 1)
                    axial = 0.5 * (high - low)
                    edge = pltpu.roll(edges, lanes - 2 * (e * cells_ax + x) - 2, 1)
                    inward = jnp.where(lane == 0, edge, pltpu.roll(centre, 1, 1))
                    outward = jnp.where(lane == lanes - 1, edge, pltpu.roll(centre, lanes - 1, 1))
                    radial = has_outer * outward - has_inner * inward
                    turned = (rate if p == 0 else -rate) * at(e, 1 - p, x)
                    for f in range(fields):
                        term = (
                            jac_axial[e, f] * axial
                            + jac_radial[e, f] * radial
                            + jac_swirl[e, f] * turned
                        )
                        if f == e:
                            term = term + centre
                        total[f] = term if e == 0 else total[f] + term
                for f in range(fields):
                    out[f, here, :] = total[f]
        return carry

    lax.fori_loop(0, half // chunk, step, 0)


def whole(shape):
    return pl.BlockSpec(shape, lambda i, where: (0,) * len(shape))


def stepped(shape):
    return pl.BlockSpec((1, *shape[1:]), lambda i, where: (i,) + (0,) * (len(shape) - 1))


def chosen(shape):
    return pl.BlockSpec((1, *shape[1:]), lambda i, where: (where[0],) + (0,) * (len(shape) - 1))


SMEM = pl.BlockSpec(memory_space=pltpu.SMEM)
ANY = pl.BlockSpec(memory_space=pl.ANY)


def call(kernel, steps, where, args, in_specs, outs, out_specs, scratch, flops):
    moved = sum(a.size * a.dtype.itemsize for a in args) + sum(o.size * o.dtype.itemsize for o in outs)
    return pl.pallas_call(
        kernel,
        grid_spec=pltpu.PrefetchScalarGridSpec(
            num_scalar_prefetch=1,
            grid=(steps,),
            in_specs=in_specs,
            out_specs=out_specs,
            scratch_shapes=scratch,
        ),
        out_shape=outs,
        compiler_params=pltpu.CompilerParams(vmem_limit_bytes=VMEM_LIMIT),
        cost_estimate=pl.CostEstimate(flops=flops, bytes_accessed=moved, transcendentals=0),
    )(where, *args)


def body(adjoint, state, wake, jac_axial, jac_radial, jac_swirl, wake_coupling):
    fields, modes, cells_ax, lanes = adjoint.shape
    groups = lax.axis_size("mode")
    count = groups * modes
    rad_size = lax.axis_size("rad")
    ax_size = lax.axis_size("ax")
    width = 2 if cells_ax % 2 == 0 else 1
    steps = cells_ax // width
    rows = modes * cells_ax
    cols = width * fields * lanes
    f32 = jnp.float32

    def cols_of(j, f):
        return pl.ds((j * fields + f) * lanes, lanes)

    dims = (fields, modes, cells_ax, width, cols_of)
    own_table, other_table, back_table = tables(groups, modes)
    where = jnp.stack([lax.axis_index("mode"), lax.axis_index("rad")]).astype(jnp.int32)

    adj = adjoint.reshape(fields, rows, lanes)
    st = state.reshape(fields, rows, lanes)
    wk = wake.reshape(rows, lanes)

    def fetch(value, s):
        return lax.ppermute(value, "mode", [((i + s) % groups, i) for i in range(groups)])

    def deliver(value, s):
        return lax.ppermute(value, "mode", [(i, (i + s) % groups) for i in range(groups)])

    adj_recv = [fetch(adj, s) for s in range(1, groups)]

    up = [(i, (i + 1) % ax_size) for i in range(ax_size)]
    down = [(i, (i - 1) % ax_size) for i in range(ax_size)]
    layer = jax.ShapeDtypeStruct((fields, modes, lanes), adjoint.dtype)
    first, last, edges = pl.pallas_call(
        functools.partial(pack_kernel, fields, modes, cells_ax),
        out_shape=[layer, layer, jax.ShapeDtypeStruct((modes, lanes), adjoint.dtype)],
        compiler_params=pltpu.CompilerParams(vmem_limit_bytes=VMEM_LIMIT),
    )(adj)
    below = lax.ppermute(last, "ax", up)
    above = lax.ppermute(first, "ax", down)
    below = jnp.where(lax.axis_index("ax") == 0, 0.0, below)
    above = jnp.where(lax.axis_index("ax") == ax_size - 1, 0.0, above)
    if rad_size == 2:
        inner = outer = lax.ppermute(edges, "rad", [(0, 1), (1, 0)])
    else:
        inner = lax.ppermute(edges, "rad", [(i, i + 1) for i in range(rad_size - 1)])
        outer = lax.ppermute(edges, "rad", [(i + 1, i) for i in range(rad_size - 1)])
    wake_recv = [fetch(wk, s) for s in range(1, groups)]

    field_shape = (fields, rows, lanes)
    angle_shape = (steps, count, cols)
    angle = jax.ShapeDtypeStruct(angle_shape, f32)
    field = jax.ShapeDtypeStruct(field_shape, f32)
    plane = jax.ShapeDtypeStruct((rows, lanes), f32)
    own_flops = 2 * 2 * 3 * count * modes * steps * cols

    a_own, c_own = call(
        functools.partial(own_kernel, dims), steps, where,
        (adj, st, wake_coupling, own_table),
        [whole(field_shape), whole(field_shape), SMEM, chosen(own_table.shape)],
        [angle, angle],
        [stepped(angle_shape), stepped(angle_shape)],
        [pltpu.VMEM((3 * modes, cols), jnp.bfloat16)] * 2,
        own_flops,
    )

    chunk = 16 if modes % 32 == 0 else 8
    base = call(
        functools.partial(
            base_kernel, fields, modes, cells_ax, chunk, count, lanes * rad_size, rad_size
        ),
        1, where,
        (adj, below, above, inner, outer, jac_axial, jac_radial, jac_swirl),
        [whole(field_shape), whole(below.shape), whole(above.shape)]
        + [whole(edges.shape)] * 2 + [SMEM] * 3,
        [field], [whole(field_shape)], [],
        32 * fields * fields * rows * lanes,
    )[0]

    cuts = (0, modes * 3 // 4 // 8 * 8, modes)
    pieces = len(cuts) - 1
    piece_rows = [(cuts[k + 1] - cuts[k]) * cells_ax for k in range(pieces)]
    joined = call(
        functools.partial(join_kernel, dims, groups, cuts), steps, where,
        (*adj_recv, a_own, c_own, other_table, base),
        [whole(field_shape)] * (groups - 1)
        + [stepped(angle_shape), stepped(angle_shape), chosen(other_table.shape), ANY],
        [angle] + [jax.ShapeDtypeStruct((n, lanes), f32) for n in piece_rows] * groups,
        [stepped(angle_shape)] + [whole((n, lanes)) for n in piece_rows] * groups,
        [pltpu.VMEM((3 * modes, cols), jnp.bfloat16)],
        (groups - 1) * own_flops // 2,
    )
    a_all = joined[0]
    parts = [joined[1 + k :: pieces] for k in range(pieces)]
    arrived = [[deliver(part[s], s) for s in range(1, groups)] for part in parts[:1]]
    if groups == 2 and rad_size == 2:
        sibling = lax.ppermute(parts[1][1], "rad", [(0, 1), (1, 0)])
        arrived.append([lax.ppermute(sibling, ("mode", "rad"), [(i, 3 - i) for i in range(4)])])
    else:
        arrived.append([deliver(parts[1][s], s) for s in range(1, groups)])

    adjoint_in = call(
        functools.partial(back_kernel, dims, groups), steps, where,
        (wk, *wake_recv, a_all, base, wake_coupling, back_table),
        [whole((rows, lanes))] * groups
        + [stepped(angle_shape), whole(field_shape), SMEM, chosen(back_table.shape)],
        [field], [whole(field_shape)],
        [pltpu.VMEM((2 * count, cols), jnp.bfloat16)],
        own_flops // 2,
    )[0]

    early, late = (functools.reduce(jnp.add, arrived[k], parts[k][0]) for k in range(pieces))
    wake_grad = -jnp.concatenate([early, late], axis=0)
    return (
        adjoint_in.reshape(adjoint.shape),
        wake_grad.reshape(wake.shape),
    )


def solution(mesh):
    return jax.shard_map(
        body,
        mesh=mesh,
        in_specs=(
            P(None, "mode", "ax", "rad"),
            P(None, "mode", "ax", "rad"),
            P("mode", "ax", "rad"),
            P(),
            P(),
            P(),
            P(),
        ),
        out_specs=(P(None, "mode", "ax", "rad"), P("mode", "ax", "rad")),
        check_vma=False,
    )
```

```python
import functools
import math

import jax
import jax.numpy as jnp
import ml_dtypes
import numpy as np
from jax import lax
from jax.experimental import pallas as pl
from jax.experimental.pallas import tpu as pltpu
from jax.sharding import PartitionSpec as P

VMEM_LIMIT = 32 * 1024 * 1024


def fourier_basis(count):
    angle = np.arange(count)[:, None]
    coef = np.arange(count)[None, :]
    phase = ((coef // 2) * angle % count) * (2.0 * math.pi / count)
    table = math.sqrt(2.0 / count) * np.where(coef % 2 == 0, np.cos(phase), np.sin(phase))
    table = np.where(coef == 0, 1.0 / math.sqrt(count), table)
    table = np.where(coef == 1, np.where(angle % 2 == 0, 1.0, -1.0) / math.sqrt(count), table)
    return table.astype(np.float32)


def three_terms(table):
    high = table.astype(ml_dtypes.bfloat16)
    low = (table - high.astype(np.float32)).astype(ml_dtypes.bfloat16)
    return np.concatenate([high, low, high], axis=-1)


def two_terms(table):
    high = table.astype(ml_dtypes.bfloat16)
    low = (table - high.astype(np.float32)).astype(ml_dtypes.bfloat16)
    return np.concatenate([high, low], axis=0)


def tables(groups, modes_here):
    count = groups * modes_here
    basis = fourier_basis(count)
    own, other, back = [], [], []
    for m in range(groups):
        rolled = np.roll(np.roll(basis, -m * modes_here, axis=0), -m * modes_here, axis=1)
        blocks = [rolled[:, s * modes_here : (s + 1) * modes_here] for s in range(groups)]
        own.append(three_terms(blocks[0]))
        other.append(np.stack([three_terms(block) for block in blocks[1:]]))
        back.append(two_terms(np.ascontiguousarray(blocks[0].T)))
    return np.stack(own), np.stack(other), np.stack(back)


def split(value):
    high = value.astype(jnp.bfloat16)
    low = (value - high.astype(jnp.float32)).astype(jnp.bfloat16)
    return high, low


def put_split(terms, row, rows, total, cols, value):
    high, low = split(value)
    terms[pl.ds(row, rows), cols] = high
    terms[pl.ds(total + row, rows), cols] = high
    terms[pl.ds(2 * total + row, rows), cols] = low


def pack_kernel(fields, modes, cells_ax, adj, first, last, edges):
    lanes = adj.shape[2]
    pair = lax.broadcasted_iota(jnp.int32, (modes, lanes), 1) // 2
    packed = jnp.zeros((modes, lanes), jnp.float32)
    for f in range(fields):
        for x in range(cells_ax):
            block = adj[f, pl.ds(x, modes, stride=cells_ax), :]
            if x == 0:
                first[f] = block
            if x == cells_ax - 1:
                last[f] = block
            j = f * cells_ax + x
            packed = jnp.where(pair == j, pltpu.roll(block, 2 * j + 1, 1), packed)
    edges[...] = packed


def own_kernel(dims, where, adj, state, coupling, table, a_out, c_out, terms_a, terms_c):
    fields, modes, cells_ax, width, cols_of = dims
    for j in range(width):
        x = pl.program_id(0) * width + j
        rows = pl.ds(x, modes, stride=cells_ax)
        for f in range(fields):
            put_split(terms_a, 0, modes, modes, cols_of(j, f), adj[f, rows, :])
    a_out[0] = jnp.dot(table[0], terms_a[...], preferred_element_type=jnp.float32)
    for j in range(width):
        x = pl.program_id(0) * width + j
        rows = pl.ds(x, modes, stride=cells_ax)
        for f in range(fields):
            mixed = coupling[f, 0] * state[0, rows, :]
            for e in range(1, fields):
                mixed = mixed + coupling[f, e] * state[e, rows, :]
            put_split(terms_c, 0, modes, modes, cols_of(j, f), mixed)
    c_out[0] = jnp.dot(table[0], terms_c[...], preferred_element_type=jnp.float32)


def join_kernel(dims, groups, cuts, where, *refs):
    fields, modes, cells_ax, width, cols_of = dims
    pieces = len(cuts) - 1
    recv = refs[: groups - 1]
    a_own, c_own, table, _, a_out = refs[groups - 1 : groups + 4]
    h_out = refs[groups + 4 : -1]
    terms = refs[-1]
    total = a_own[0]
    for s in range(groups - 1):
        for j in range(width):
            x = pl.program_id(0) * width + j
            rows = pl.ds(x, modes, stride=cells_ax)
            for f in range(fields):
                put_split(terms, 0, modes, modes, cols_of(j, f), recv[s][f, rows, :])
        total = total + jnp.dot(table[0, s], terms[...], preferred_element_type=jnp.float32)
    a_out[0] = total
    for j in range(width):
        x = pl.program_id(0) * width + j
        for s, k in ((s, k) for s in range(groups) for k in range(pieces)):
            here = pl.ds(s * modes + cuts[k], cuts[k + 1] - cuts[k])
            rows = pl.ds(x, cuts[k + 1] - cuts[k], stride=cells_ax)
            part = a_out[0, here, cols_of(j, 0)] * c_own[0, here, cols_of(j, 0)]
            for f in range(1, fields):
                part = part + a_out[0, here, cols_of(j, f)] * c_own[0, here, cols_of(j, f)]
            h_out[s * pieces + k][rows, :] = part


def back_kernel(dims, groups, where, *refs):
    fields, modes, cells_ax, width, cols_of = dims
    wakes = refs[:groups]
    angle, base, coupling, table, out, terms = refs[groups:]
    count = groups * modes
    for j in range(width):
        x = pl.program_id(0) * width + j
        rows = pl.ds(x, modes, stride=cells_ax)
        for s in range(groups):
            wake = wakes[s][rows, :]
            for f in range(fields):
                scaled = wake * angle[0, pl.ds(s * modes, modes), cols_of(j, f)]
                high, low = split(scaled)
                terms[pl.ds(s * modes, modes), cols_of(j, f)] = high
                terms[pl.ds(count + s * modes, modes), cols_of(j, f)] = low
    both = jnp.dot(table[0], terms[pl.ds(0, count), :], preferred_element_type=jnp.float32)
    rest = jnp.dot(
        table[0, pl.ds(0, modes), :], terms[pl.ds(count, count), :], preferred_element_type=jnp.float32
    )
    returned = both[:modes] + (both[modes:] + rest)
    for j in range(width):
        x = pl.program_id(0) * width + j
        rows = pl.ds(x, modes, stride=cells_ax)
        for f in range(fields):
            value = base[f, rows, :]
            for e in range(fields):
                value = value - coupling[e, f] * returned[:, cols_of(j, e)]
            out[f, rows, :] = value


def base_kernel(
    fields, modes, cells_ax, chunk, mode_total, rad_total, rad_size,
    where, adj, below, above, inner, outer, jac_axial, jac_radial, jac_swirl, out,
):
    lanes = adj.shape[2]
    half = modes // 2
    rad = where[1]
    lane = lax.broadcasted_iota(jnp.int32, (chunk, lanes), 1)
    row = lax.broadcasted_iota(jnp.int32, (chunk, lanes), 0)
    radius = 0.5 + ((rad * lanes + lane).astype(jnp.float32) + 0.5) / jnp.float32(2.0 * rad_total)
    swirl = 0.25 / radius
    has_inner = jnp.where((lane == 0) & (rad == 0), 0.0, 0.5)
    has_outer = jnp.where((lane == lanes - 1) & (rad == rad_size - 1), 0.0, 0.5)

    def step(i, carry):
        order = (where[0] * half + i * chunk + row).astype(jnp.float32) / jnp.float32(mode_total // 2)
        rate = swirl * order
        for p in range(2):
            halo = pl.ds(2 * i * chunk + p, chunk, stride=2)
            edges = jnp.where(lane % 2 == 0, pltpu.roll(inner[halo, :], 2, 1), outer[halo, :])
            for x in range(cells_ax):
                def at(e, parity, cell):
                    start = (2 * i * chunk + parity) * cells_ax + cell
                    return adj[e, pl.ds(start, chunk, stride=2 * cells_ax), :]

                here = pl.ds((2 * i * chunk + p) * cells_ax + x, chunk, stride=2 * cells_ax)
                total = [None] * fields
                for e in range(fields):
                    centre = at(e, p, x)
                    low = below[e, halo, :] if x == 0 else at(e, p, x - 1)
                    high = above[e, halo, :] if x == cells_ax - 1 else at(e, p, x + 1)
                    axial = 0.5 * (high - low)
                    edge = pltpu.roll(edges, lanes - 2 * (e * cells_ax + x) - 2, 1)
                    inward = jnp.where(lane == 0, edge, pltpu.roll(centre, 1, 1))
                    outward = jnp.where(lane == lanes - 1, edge, pltpu.roll(centre, lanes - 1, 1))
                    radial = has_outer * outward - has_inner * inward
                    turned = (rate if p == 0 else -rate) * at(e, 1 - p, x)
                    for f in range(fields):
                        term = (
                            jac_axial[e, f] * axial
                            + jac_radial[e, f] * radial
                            + jac_swirl[e, f] * turned
                        )
                        if f == e:
                            term = term + centre
                        total[f] = term if e == 0 else total[f] + term
                for f in range(fields):
                    out[f, here, :] = total[f]
        return carry

    lax.fori_loop(0, half // chunk, step, 0)


def whole(shape):
    return pl.BlockSpec(shape, lambda i, where: (0,) * len(shape))


def stepped(shape):
    return pl.BlockSpec((1, *shape[1:]), lambda i, where: (i,) + (0,) * (len(shape) - 1))


def chosen(shape):
    return pl.BlockSpec((1, *shape[1:]), lambda i, where: (where[0],) + (0,) * (len(shape) - 1))


SMEM = pl.BlockSpec(memory_space=pltpu.SMEM)
ANY = pl.BlockSpec(memory_space=pl.ANY)


def call(kernel, steps, where, args, in_specs, outs, out_specs, scratch, flops):
    moved = sum(a.size * a.dtype.itemsize for a in args) + sum(o.size * o.dtype.itemsize for o in outs)
    return pl.pallas_call(
        kernel,
        grid_spec=pltpu.PrefetchScalarGridSpec(
            num_scalar_prefetch=1,
            grid=(steps,),
            in_specs=in_specs,
            out_specs=out_specs,
            scratch_shapes=scratch,
        ),
        out_shape=outs,
        compiler_params=pltpu.CompilerParams(vmem_limit_bytes=VMEM_LIMIT),
        cost_estimate=pl.CostEstimate(flops=flops, bytes_accessed=moved, transcendentals=0),
    )(where, *args)


def body(adjoint, state, wake, jac_axial, jac_radial, jac_swirl, wake_coupling):
    fields, modes, cells_ax, lanes = adjoint.shape
    groups = lax.axis_size("mode")
    count = groups * modes
    rad_size = lax.axis_size("rad")
    ax_size = lax.axis_size("ax")
    width = 2 if cells_ax % 2 == 0 else 1
    steps = cells_ax // width
    rows = modes * cells_ax
    cols = width * fields * lanes
    f32 = jnp.float32

    def cols_of(j, f):
        return pl.ds((j * fields + f) * lanes, lanes)

    dims = (fields, modes, cells_ax, width, cols_of)
    own_table, other_table, back_table = tables(groups, modes)
    where = jnp.stack([lax.axis_index("mode"), lax.axis_index("rad")]).astype(jnp.int32)

    adj = adjoint.reshape(fields, rows, lanes)
    st = state.reshape(fields, rows, lanes)
    wk = wake.reshape(rows, lanes)

    def fetch(value, s):
        return lax.ppermute(value, "mode", [((i + s) % groups, i) for i in range(groups)])

    def deliver(value, s):
        return lax.ppermute(value, "mode", [(i, (i + s) % groups) for i in range(groups)])

    adj_recv = [fetch(adj, s) for s in range(1, groups)]

    up = [(i, (i + 1) % ax_size) for i in range(ax_size)]
    down = [(i, (i - 1) % ax_size) for i in range(ax_size)]
    layer = jax.ShapeDtypeStruct((fields, modes, lanes), adjoint.dtype)
    first, last, edges = pl.pallas_call(
        functools.partial(pack_kernel, fields, modes, cells_ax),
        out_shape=[layer, layer, jax.ShapeDtypeStruct((modes, lanes), adjoint.dtype)],
        compiler_params=pltpu.CompilerParams(vmem_limit_bytes=VMEM_LIMIT),
    )(adj)
    below = lax.ppermute(last, "ax", up)
    above = lax.ppermute(first, "ax", down)
    below = jnp.where(lax.axis_index("ax") == 0, 0.0, below)
    above = jnp.where(lax.axis_index("ax") == ax_size - 1, 0.0, above)
    if rad_size == 2:
        inner = outer = lax.ppermute(edges, "rad", [(0, 1), (1, 0)])
    else:
        inner = lax.ppermute(edges, "rad", [(i, i + 1) for i in range(rad_size - 1)])
        outer = lax.ppermute(edges, "rad", [(i + 1, i) for i in range(rad_size - 1)])
    if groups == 2 and rad_size == 2:
        sibling_wake = lax.ppermute(wk, "rad", [(0, 1), (1, 0)])
        wake_recv = [lax.ppermute(sibling_wake, ("mode", "rad"), [(i, 3 - i) for i in range(4)])]
    else:
        wake_recv = [fetch(wk, s) for s in range(1, groups)]

    field_shape = (fields, rows, lanes)
    angle_shape = (steps, count, cols)
    angle = jax.ShapeDtypeStruct(angle_shape, f32)
    field = jax.ShapeDtypeStruct(field_shape, f32)
    plane = jax.ShapeDtypeStruct((rows, lanes), f32)
    own_flops = 2 * 2 * 3 * count * modes * steps * cols

    a_own, c_own = call(
        functools.partial(own_kernel, dims), steps, where,
        (adj, st, wake_coupling, own_table),
        [whole(field_shape), whole(field_shape), SMEM, chosen(own_table.shape)],
        [angle, angle],
        [stepped(angle_shape), stepped(angle_shape)],
        [pltpu.VMEM((3 * modes, cols), jnp.bfloat16)] * 2,
        own_flops,
    )

    chunk = 16 if modes % 32 == 0 else 8
    base = call(
        functools.partial(
            base_kernel, fields, modes, cells_ax, chunk, count, lanes * rad_size, rad_size
        ),
        1, where,
        (adj, below, above, inner, outer, jac_axial, jac_radial, jac_swirl),
        [whole(field_shape), whole(below.shape), whole(above.shape)]
        + [whole(edges.shape)] * 2 + [SMEM] * 3,
        [field], [whole(field_shape)], [],
        32 * fields * fields * rows * lanes,
    )[0]

    cuts = (0, modes * 3 // 4 // 8 * 8, modes)
    pieces = len(cuts) - 1
    piece_rows = [(cuts[k + 1] - cuts[k]) * cells_ax for k in range(pieces)]
    joined = call(
        functools.partial(join_kernel, dims, groups, cuts), steps, where,
        (*adj_recv, a_own, c_own, other_table, base),
        [whole(field_shape)] * (groups - 1)
        + [stepped(angle_shape), stepped(angle_shape), chosen(other_table.shape), ANY],
        [angle] + [jax.ShapeDtypeStruct((n, lanes), f32) for n in piece_rows] * groups,
        [stepped(angle_shape)] + [whole((n, lanes)) for n in piece_rows] * groups,
        [pltpu.VMEM((3 * modes, cols), jnp.bfloat16)],
        (groups - 1) * own_flops // 2,
    )
    a_all = joined[0]
    parts = [joined[1 + k :: pieces] for k in range(pieces)]
    arrived = [[deliver(part[s], s) for s in range(1, groups)] for part in parts[:1]]
    if groups == 2 and rad_size == 2:
        sibling = lax.ppermute(parts[1][1], "rad", [(0, 1), (1, 0)])
        arrived.append([lax.ppermute(sibling, ("mode", "rad"), [(i, 3 - i) for i in range(4)])])
    else:
        arrived.append([deliver(parts[1][s], s) for s in range(1, groups)])

    adjoint_in = call(
        functools.partial(back_kernel, dims, groups), steps, where,
        (wk, *wake_recv, a_all, base, wake_coupling, back_table),
        [whole((rows, lanes))] * groups
        + [stepped(angle_shape), whole(field_shape), SMEM, chosen(back_table.shape)],
        [field], [whole(field_shape)],
        [pltpu.VMEM((2 * count, cols), jnp.bfloat16)],
        own_flops // 2,
    )[0]

    early, late = (functools.reduce(jnp.add, arrived[k], parts[k][0]) for k in range(pieces))
    wake_grad = -jnp.concatenate([early, late], axis=0)
    return (
        adjoint_in.reshape(adjoint.shape),
        wake_grad.reshape(wake.shape),
    )


def solution(mesh):
    return jax.shard_map(
        body,
        mesh=mesh,
        in_specs=(
            P(None, "mode", "ax", "rad"),
            P(None, "mode", "ax", "rad"),
            P("mode", "ax", "rad"),
            P(),
            P(),
            P(),
            P(),
        ),
        out_specs=(P(None, "mode", "ax", "rad"), P("mode", "ax", "rad")),
        check_vma=False,
    )
```

```python
import functools
import math

import jax
import jax.numpy as jnp
import ml_dtypes
import numpy as np
from jax import lax
from jax.experimental import pallas as pl
from jax.experimental.pallas import tpu as pltpu
from jax.sharding import PartitionSpec as P

VMEM_LIMIT = 32 * 1024 * 1024


def fourier_basis(count):
    angle = np.arange(count)[:, None]
    coef = np.arange(count)[None, :]
    phase = ((coef // 2) * angle % count) * (2.0 * math.pi / count)
    table = math.sqrt(2.0 / count) * np.where(coef % 2 == 0, np.cos(phase), np.sin(phase))
    table = np.where(coef == 0, 1.0 / math.sqrt(count), table)
    table = np.where(coef == 1, np.where(angle % 2 == 0, 1.0, -1.0) / math.sqrt(count), table)
    return table.astype(np.float32)


def three_terms(table):
    high = table.astype(ml_dtypes.bfloat16)
    low = (table - high.astype(np.float32)).astype(ml_dtypes.bfloat16)
    return np.concatenate([high, low, high], axis=-1)


def two_terms(table):
    high = table.astype(ml_dtypes.bfloat16)
    low = (table - high.astype(np.float32)).astype(ml_dtypes.bfloat16)
    return np.concatenate([high, low], axis=0)


def tables(groups, modes_here):
    count = groups * modes_here
    basis = fourier_basis(count)
    own, other, back = [], [], []
    for m in range(groups):
        rolled = np.roll(np.roll(basis, -m * modes_here, axis=0), -m * modes_here, axis=1)
        blocks = [rolled[:, s * modes_here : (s + 1) * modes_here] for s in range(groups)]
        own.append(three_terms(blocks[0]))
        other.append(np.stack([three_terms(block) for block in blocks[1:]]))
        back.append(two_terms(np.ascontiguousarray(blocks[0].T)))
    return np.stack(own), np.stack(other), np.stack(back)


def split(value):
    high = value.astype(jnp.bfloat16)
    low = (value - high.astype(jnp.float32)).astype(jnp.bfloat16)
    return high, low


def put_split(terms, row, rows, total, cols, value):
    high, low = split(value)
    terms[pl.ds(row, rows), cols] = high
    terms[pl.ds(total + row, rows), cols] = high
    terms[pl.ds(2 * total + row, rows), cols] = low


def pack_kernel(fields, modes, cells_ax, adj, first, last, edges):
    lanes = adj.shape[2]
    pair = lax.broadcasted_iota(jnp.int32, (modes, lanes), 1) // 2
    packed = jnp.zeros((modes, lanes), jnp.float32)
    for f in range(fields):
        for x in range(cells_ax):
            block = adj[f, pl.ds(x, modes, stride=cells_ax), :]
            if x == 0:
                first[f] = block
            if x == cells_ax - 1:
                last[f] = block
            j = f * cells_ax + x
            packed = jnp.where(pair == j, pltpu.roll(block, 2 * j + 1, 1), packed)
    edges[...] = packed


def own_kernel(dims, where, adj, state, coupling, table, a_out, c_out, terms_a, terms_c):
    fields, modes, cells_ax, width, cols_of = dims
    for j in range(width):
        x = pl.program_id(0) * width + j
        rows = pl.ds(x, modes, stride=cells_ax)
        for f in range(fields):
            put_split(terms_a, 0, modes, modes, cols_of(j, f), adj[f, rows, :])
    a_out[0] = jnp.dot(table[0], terms_a[...], preferred_element_type=jnp.float32)
    for j in range(width):
        x = pl.program_id(0) * width + j
        rows = pl.ds(x, modes, stride=cells_ax)
        for f in range(fields):
            mixed = coupling[f, 0] * state[0, rows, :]
            for e in range(1, fields):
                mixed = mixed + coupling[f, e] * state[e, rows, :]
            put_split(terms_c, 0, modes, modes, cols_of(j, f), mixed)
    c_out[0] = jnp.dot(table[0], terms_c[...], preferred_element_type=jnp.float32)


def join_kernel(dims, groups, cuts, where, *refs):
    fields, modes, cells_ax, width, cols_of = dims
    pieces = len(cuts) - 1
    recv = refs[: groups - 1]
    a_own, c_own, table, _, a_out = refs[groups - 1 : groups + 4]
    h_out = refs[groups + 4 : -1]
    terms = refs[-1]
    total = a_own[0]
    for s in range(groups - 1):
        for j in range(width):
            x = pl.program_id(0) * width + j
            rows = pl.ds(x, modes, stride=cells_ax)
            for f in range(fields):
                put_split(terms, 0, modes, modes, cols_of(j, f), recv[s][f, rows, :])
        total = total + jnp.dot(table[0, s], terms[...], preferred_element_type=jnp.float32)
    a_out[0] = total
    for j in range(width):
        x = pl.program_id(0) * width + j
        for s, k in ((s, k) for s in range(groups) for k in range(pieces)):
            here = pl.ds(s * modes + cuts[k], cuts[k + 1] - cuts[k])
            rows = pl.ds(x, cuts[k + 1] - cuts[k], stride=cells_ax)
            part = a_out[0, here, cols_of(j, 0)] * c_own[0, here, cols_of(j, 0)]
            for f in range(1, fields):
                part = part + a_out[0, here, cols_of(j, f)] * c_own[0, here, cols_of(j, f)]
            h_out[s * pieces + k][rows, :] = part


def back_kernel(dims, groups, where, *refs):
    fields, modes, cells_ax, width, cols_of = dims
    wakes = refs[:groups]
    angle, base, coupling, table, out, terms = refs[groups:]
    count = groups * modes
    for j in range(width):
        x = pl.program_id(0) * width + j
        rows = pl.ds(x, modes, stride=cells_ax)
        for s in range(groups):
            wake = wakes[s][rows, :]
            for f in range(fields):
                scaled = wake * angle[0, pl.ds(s * modes, modes), cols_of(j, f)]
                high, low = split(scaled)
                terms[pl.ds(s * modes, modes), cols_of(j, f)] = high
                terms[pl.ds(count + s * modes, modes), cols_of(j, f)] = low
    both = jnp.dot(table[0], terms[pl.ds(0, count), :], preferred_element_type=jnp.float32)
    rest = jnp.dot(
        table[0, pl.ds(0, modes), :], terms[pl.ds(count, count), :], preferred_element_type=jnp.float32
    )
    returned = both[:modes] + (both[modes:] + rest)
    for j in range(width):
        x = pl.program_id(0) * width + j
        rows = pl.ds(x, modes, stride=cells_ax)
        for f in range(fields):
            value = base[f, rows, :]
            for e in range(fields):
                value = value - coupling[e, f] * returned[:, cols_of(j, e)]
            out[f, rows, :] = value


def base_kernel(
    fields, modes, cells_ax, chunk, mode_total, rad_total, rad_size,
    where, adj, below, above, inner, outer, jac_axial, jac_radial, jac_swirl, out,
):
    lanes = adj.shape[2]
    half = modes // 2
    rad = where[1]
    lane = lax.broadcasted_iota(jnp.int32, (chunk, lanes), 1)
    row = lax.broadcasted_iota(jnp.int32, (chunk, lanes), 0)
    radius = 0.5 + ((rad * lanes + lane).astype(jnp.float32) + 0.5) / jnp.float32(2.0 * rad_total)
    swirl = 0.25 / radius
    has_inner = jnp.where((lane == 0) & (rad == 0), 0.0, 0.5)
    has_outer = jnp.where((lane == lanes - 1) & (rad == rad_size - 1), 0.0, 0.5)

    def step(i, carry):
        order = (where[0] * half + i * chunk + row).astype(jnp.float32) / jnp.float32(mode_total // 2)
        rate = swirl * order
        for p in range(2):
            halo = pl.ds(2 * i * chunk + p, chunk, stride=2)
            edges = jnp.where(lane % 2 == 0, pltpu.roll(inner[halo, :], 2, 1), outer[halo, :])
            for x in range(cells_ax):
                def at(e, parity, cell):
                    start = (2 * i * chunk + parity) * cells_ax + cell
                    return adj[e, pl.ds(start, chunk, stride=2 * cells_ax), :]

                here = pl.ds((2 * i * chunk + p) * cells_ax + x, chunk, stride=2 * cells_ax)
                total = [None] * fields
                for e in range(fields):
                    centre = at(e, p, x)
                    low = below[e, halo, :] if x == 0 else at(e, p, x - 1)
                    high = above[e, halo, :] if x == cells_ax - 1 else at(e, p, x + 1)
                    axial = 0.5 * (high - low)
                    edge = pltpu.roll(edges, lanes - 2 * (e * cells_ax + x) - 2, 1)
                    inward = jnp.where(lane == 0, edge, pltpu.roll(centre, 1, 1))
                    outward = jnp.where(lane == lanes - 1, edge, pltpu.roll(centre, lanes - 1, 1))
                    radial = has_outer * outward - has_inner * inward
                    turned = (rate if p == 0 else -rate) * at(e, 1 - p, x)
                    for f in range(fields):
                        term = (
                            jac_axial[e, f] * axial
                            + jac_radial[e, f] * radial
                            + jac_swirl[e, f] * turned
                        )
                        if f == e:
                            term = term + centre
                        total[f] = term if e == 0 else total[f] + term
                for f in range(fields):
                    out[f, here, :] = total[f]
        return carry

    lax.fori_loop(0, half // chunk, step, 0)


def whole(shape):
    return pl.BlockSpec(shape, lambda i, where: (0,) * len(shape))


def stepped(shape):
    return pl.BlockSpec((1, *shape[1:]), lambda i, where: (i,) + (0,) * (len(shape) - 1))


def chosen(shape):
    return pl.BlockSpec((1, *shape[1:]), lambda i, where: (where[0],) + (0,) * (len(shape) - 1))


SMEM = pl.BlockSpec(memory_space=pltpu.SMEM)
ANY = pl.BlockSpec(memory_space=pl.ANY)


def call(kernel, steps, where, args, in_specs, outs, out_specs, scratch, flops):
    moved = sum(a.size * a.dtype.itemsize for a in args) + sum(o.size * o.dtype.itemsize for o in outs)
    return pl.pallas_call(
        kernel,
        grid_spec=pltpu.PrefetchScalarGridSpec(
            num_scalar_prefetch=1,
            grid=(steps,),
            in_specs=in_specs,
            out_specs=out_specs,
            scratch_shapes=scratch,
        ),
        out_shape=outs,
        compiler_params=pltpu.CompilerParams(vmem_limit_bytes=VMEM_LIMIT),
        cost_estimate=pl.CostEstimate(flops=flops, bytes_accessed=moved, transcendentals=0),
    )(where, *args)


def body(adjoint, state, wake, jac_axial, jac_radial, jac_swirl, wake_coupling):
    fields, modes, cells_ax, lanes = adjoint.shape
    groups = lax.axis_size("mode")
    count = groups * modes
    rad_size = lax.axis_size("rad")
    ax_size = lax.axis_size("ax")
    width = 2 if cells_ax % 2 == 0 else 1
    steps = cells_ax // width
    rows = modes * cells_ax
    cols = width * fields * lanes
    f32 = jnp.float32

    def cols_of(j, f):
        return pl.ds((j * fields + f) * lanes, lanes)

    dims = (fields, modes, cells_ax, width, cols_of)
    own_table, other_table, back_table = tables(groups, modes)
    where = jnp.stack([lax.axis_index("mode"), lax.axis_index("rad")]).astype(jnp.int32)

    adj = adjoint.reshape(fields, rows, lanes)
    st = state.reshape(fields, rows, lanes)
    wk = wake.reshape(rows, lanes)

    def fetch(value, s):
        return lax.ppermute(value, "mode", [((i + s) % groups, i) for i in range(groups)])

    def deliver(value, s):
        return lax.ppermute(value, "mode", [(i, (i + s) % groups) for i in range(groups)])

    adj_recv = [fetch(adj, s) for s in range(1, groups)]

    up = [(i, (i + 1) % ax_size) for i in range(ax_size)]
    down = [(i, (i - 1) % ax_size) for i in range(ax_size)]
    layer = jax.ShapeDtypeStruct((fields, modes, lanes), adjoint.dtype)
    first, last, edges = pl.pallas_call(
        functools.partial(pack_kernel, fields, modes, cells_ax),
        out_shape=[layer, layer, jax.ShapeDtypeStruct((modes, lanes), adjoint.dtype)],
        compiler_params=pltpu.CompilerParams(vmem_limit_bytes=VMEM_LIMIT),
    )(adj)
    below = lax.ppermute(last, "ax", up)
    above = lax.ppermute(first, "ax", down)
    below = jnp.where(lax.axis_index("ax") == 0, 0.0, below)
    above = jnp.where(lax.axis_index("ax") == ax_size - 1, 0.0, above)
    if rad_size == 2:
        inner = outer = lax.ppermute(edges, "rad", [(0, 1), (1, 0)])
    else:
        inner = lax.ppermute(edges, "rad", [(i, i + 1) for i in range(rad_size - 1)])
        outer = lax.ppermute(edges, "rad", [(i + 1, i) for i in range(rad_size - 1)])
    wake_recv = [fetch(wk, s) for s in range(1, groups)]

    field_shape = (fields, rows, lanes)
    angle_shape = (steps, count, cols)
    angle = jax.ShapeDtypeStruct(angle_shape, f32)
    field = jax.ShapeDtypeStruct(field_shape, f32)
    plane = jax.ShapeDtypeStruct((rows, lanes), f32)
    own_flops = 2 * 2 * 3 * count * modes * steps * cols

    a_own, c_own = call(
        functools.partial(own_kernel, dims), steps, where,
        (adj, st, wake_coupling, own_table),
        [whole(field_shape), whole(field_shape), SMEM, chosen(own_table.shape)],
        [angle, angle],
        [stepped(angle_shape), stepped(angle_shape)],
        [pltpu.VMEM((3 * modes, cols), jnp.bfloat16)] * 2,
        own_flops,
    )

    chunk = 16 if modes % 32 == 0 else 8
    base = call(
        functools.partial(
            base_kernel, fields, modes, cells_ax, chunk, count, lanes * rad_size, rad_size
        ),
        1, where,
        (adj, below, above, inner, outer, jac_axial, jac_radial, jac_swirl),
        [whole(field_shape), whole(below.shape), whole(above.shape)]
        + [whole(edges.shape)] * 2 + [SMEM] * 3,
        [field], [whole(field_shape)], [],
        32 * fields * fields * rows * lanes,
    )[0]

    cuts = (0, modes * 13 // 16 // 8 * 8, modes)
    pieces = len(cuts) - 1
    piece_rows = [(cuts[k + 1] - cuts[k]) * cells_ax for k in range(pieces)]
    joined = call(
        functools.partial(join_kernel, dims, groups, cuts), steps, where,
        (*adj_recv, a_own, c_own, other_table, base),
        [whole(field_shape)] * (groups - 1)
        + [stepped(angle_shape), stepped(angle_shape), chosen(other_table.shape), ANY],
        [angle] + [jax.ShapeDtypeStruct((n, lanes), f32) for n in piece_rows] * groups,
        [stepped(angle_shape)] + [whole((n, lanes)) for n in piece_rows] * groups,
        [pltpu.VMEM((3 * modes, cols), jnp.bfloat16)],
        (groups - 1) * own_flops // 2,
    )
    a_all = joined[0]
    parts = [joined[1 + k :: pieces] for k in range(pieces)]
    arrived = [[deliver(part[s], s) for s in range(1, groups)] for part in parts[:1]]
    if groups == 2 and rad_size == 2:
        sibling = lax.ppermute(parts[1][1], "rad", [(0, 1), (1, 0)])
        arrived.append([lax.ppermute(sibling, ("mode", "rad"), [(i, 3 - i) for i in range(4)])])
    else:
        arrived.append([deliver(parts[1][s], s) for s in range(1, groups)])

    adjoint_in = call(
        functools.partial(back_kernel, dims, groups), steps, where,
        (wk, *wake_recv, a_all, base, wake_coupling, back_table),
        [whole((rows, lanes))] * groups
        + [stepped(angle_shape), whole(field_shape), SMEM, chosen(back_table.shape)],
        [field], [whole(field_shape)],
        [pltpu.VMEM((2 * count, cols), jnp.bfloat16)],
        own_flops // 2,
    )[0]

    early, late = (functools.reduce(jnp.add, arrived[k], parts[k][0]) for k in range(pieces))
    wake_grad = -jnp.concatenate([early, late], axis=0)
    return (
        adjoint_in.reshape(adjoint.shape),
        wake_grad.reshape(wake.shape),
    )


def solution(mesh):
    return jax.shard_map(
        body,
        mesh=mesh,
        in_specs=(
            P(None, "mode", "ax", "rad"),
            P(None, "mode", "ax", "rad"),
            P("mode", "ax", "rad"),
            P(),
            P(),
            P(),
            P(),
        ),
        out_specs=(P(None, "mode", "ax", "rad"), P("mode", "ax", "rad")),
        check_vma=False,
    )
```

```python
import functools
import math

import jax
import jax.numpy as jnp
import ml_dtypes
import numpy as np
from jax import lax
from jax.experimental import pallas as pl
from jax.experimental.pallas import tpu as pltpu
from jax.sharding import PartitionSpec as P

VMEM_LIMIT = 32 * 1024 * 1024


def fourier_basis(count):
    angle = np.arange(count)[:, None]
    coef = np.arange(count)[None, :]
    phase = ((coef // 2) * angle % count) * (2.0 * math.pi / count)
    table = math.sqrt(2.0 / count) * np.where(coef % 2 == 0, np.cos(phase), np.sin(phase))
    table = np.where(coef == 0, 1.0 / math.sqrt(count), table)
    table = np.where(coef == 1, np.where(angle % 2 == 0, 1.0, -1.0) / math.sqrt(count), table)
    return table.astype(np.float32)


def three_terms(table):
    high = table.astype(ml_dtypes.bfloat16)
    low = (table - high.astype(np.float32)).astype(ml_dtypes.bfloat16)
    return np.concatenate([high, low, high], axis=-1)


def two_terms(table):
    high = table.astype(ml_dtypes.bfloat16)
    low = (table - high.astype(np.float32)).astype(ml_dtypes.bfloat16)
    return np.concatenate([high, low], axis=0)


def tables(groups, modes_here):
    count = groups * modes_here
    basis = fourier_basis(count)
    own, other, back = [], [], []
    for m in range(groups):
        rolled = np.roll(np.roll(basis, -m * modes_here, axis=0), -m * modes_here, axis=1)
        blocks = [rolled[:, s * modes_here : (s + 1) * modes_here] for s in range(groups)]
        own.append(three_terms(blocks[0]))
        other.append(np.stack([three_terms(block) for block in blocks[1:]]))
        back.append(two_terms(np.ascontiguousarray(blocks[0].T)))
    return np.stack(own), np.stack(other), np.stack(back)


def split(value):
    high = value.astype(jnp.bfloat16)
    low = (value - high.astype(jnp.float32)).astype(jnp.bfloat16)
    return high, low


def put_split(terms, row, rows, total, cols, value):
    high, low = split(value)
    terms[pl.ds(row, rows), cols] = high
    terms[pl.ds(total + row, rows), cols] = high
    terms[pl.ds(2 * total + row, rows), cols] = low


def pack_kernel(fields, modes, cells_ax, adj, first, last, edges):
    lanes = adj.shape[2]
    pair = lax.broadcasted_iota(jnp.int32, (modes, lanes), 1) // 2
    packed = jnp.zeros((modes, lanes), jnp.float32)
    for f in range(fields):
        for x in range(cells_ax):
            block = adj[f, pl.ds(x, modes, stride=cells_ax), :]
            if x == 0:
                first[f] = block
            if x == cells_ax - 1:
                last[f] = block
            j = f * cells_ax + x
            packed = jnp.where(pair == j, pltpu.roll(block, 2 * j + 1, 1), packed)
    edges[...] = packed


def own_kernel(dims, where, adj, state, coupling, table, a_out, c_out, terms_a, terms_c):
    fields, modes, cells_ax, width, cols_of = dims
    for j in range(width):
        x = pl.program_id(0) * width + j
        rows = pl.ds(x, modes, stride=cells_ax)
        for f in range(fields):
            put_split(terms_a, 0, modes, modes, cols_of(j, f), adj[f, rows, :])
    a_out[0] = jnp.dot(table[0], terms_a[...], preferred_element_type=jnp.float32)
    for j in range(width):
        x = pl.program_id(0) * width + j
        rows = pl.ds(x, modes, stride=cells_ax)
        for f in range(fields):
            mixed = coupling[f, 0] * state[0, rows, :]
            for e in range(1, fields):
                mixed = mixed + coupling[f, e] * state[e, rows, :]
            put_split(terms_c, 0, modes, modes, cols_of(j, f), mixed)
    c_out[0] = jnp.dot(table[0], terms_c[...], preferred_element_type=jnp.float32)


def join_kernel(dims, groups, cuts, where, *refs):
    fields, modes, cells_ax, width, cols_of = dims
    pieces = len(cuts) - 1
    recv = refs[: groups - 1]
    a_own, c_own, table, _, a_out = refs[groups - 1 : groups + 4]
    h_out = refs[groups + 4 : -1]
    terms = refs[-1]
    total = a_own[0]
    for s in range(groups - 1):
        for j in range(width):
            x = pl.program_id(0) * width + j
            rows = pl.ds(x, modes, stride=cells_ax)
            for f in range(fields):
                put_split(terms, 0, modes, modes, cols_of(j, f), recv[s][f, rows, :])
        total = total + jnp.dot(table[0, s], terms[...], preferred_element_type=jnp.float32)
    a_out[0] = total
    for j in range(width):
        x = pl.program_id(0) * width + j
        for s, k in ((s, k) for s in range(groups) for k in range(pieces)):
            here = pl.ds(s * modes + cuts[k], cuts[k + 1] - cuts[k])
            rows = pl.ds(x, cuts[k + 1] - cuts[k], stride=cells_ax)
            part = a_out[0, here, cols_of(j, 0)] * c_own[0, here, cols_of(j, 0)]
            for f in range(1, fields):
                part = part + a_out[0, here, cols_of(j, f)] * c_own[0, here, cols_of(j, f)]
            h_out[s * pieces + k][rows, :] = part


def back_kernel(dims, groups, where, *refs):
    fields, modes, cells_ax, width, cols_of = dims
    wakes = refs[:groups]
    angle, base, coupling, table, out, terms = refs[groups:]
    count = groups * modes
    for j in range(width):
        x = pl.program_id(0) * width + j
        rows = pl.ds(x, modes, stride=cells_ax)
        for s in range(groups):
            wake = wakes[s][rows, :]
            for f in range(fields):
                scaled = wake * angle[0, pl.ds(s * modes, modes), cols_of(j, f)]
                high, low = split(scaled)
                terms[pl.ds(s * modes, modes), cols_of(j, f)] = high
                terms[pl.ds(count + s * modes, modes), cols_of(j, f)] = low
    both = jnp.dot(table[0], terms[pl.ds(0, count), :], preferred_element_type=jnp.float32)
    rest = jnp.dot(
        table[0, pl.ds(0, modes), :], terms[pl.ds(count, count), :], preferred_element_type=jnp.float32
    )
    returned = both[:modes] + (both[modes:] + rest)
    for j in range(width):
        x = pl.program_id(0) * width + j
        rows = pl.ds(x, modes, stride=cells_ax)
        for f in range(fields):
            value = base[f, rows, :]
            for e in range(fields):
                value = value - coupling[e, f] * returned[:, cols_of(j, e)]
            out[f, rows, :] = value


def base_kernel(
    fields, modes, cells_ax, chunk, mode_total, rad_total, rad_size,
    where, adj, below, above, inner, outer, jac_axial, jac_radial, jac_swirl, out,
):
    lanes = adj.shape[2]
    half = modes // 2
    rad = where[1]
    lane = lax.broadcasted_iota(jnp.int32, (chunk, lanes), 1)
    row = lax.broadcasted_iota(jnp.int32, (chunk, lanes), 0)
    radius = 0.5 + ((rad * lanes + lane).astype(jnp.float32) + 0.5) / jnp.float32(2.0 * rad_total)
    swirl = 0.25 / radius
    has_inner = jnp.where((lane == 0) & (rad == 0), 0.0, 0.5)
    has_outer = jnp.where((lane == lanes - 1) & (rad == rad_size - 1), 0.0, 0.5)

    def step(i, carry):
        order = (where[0] * half + i * chunk + row).astype(jnp.float32) / jnp.float32(mode_total // 2)
        rate = swirl * order
        for p in range(2):
            halo = pl.ds(2 * i * chunk + p, chunk, stride=2)
            edges = jnp.where(lane % 2 == 0, pltpu.roll(inner[halo, :], 2, 1), outer[halo, :])
            for x in range(cells_ax):
                def at(e, parity, cell):
                    start = (2 * i * chunk + parity) * cells_ax + cell
                    return adj[e, pl.ds(start, chunk, stride=2 * cells_ax), :]

                here = pl.ds((2 * i * chunk + p) * cells_ax + x, chunk, stride=2 * cells_ax)
                total = [None] * fields
                for e in range(fields):
                    centre = at(e, p, x)
                    low = below[e, halo, :] if x == 0 else at(e, p, x - 1)
                    high = above[e, halo, :] if x == cells_ax - 1 else at(e, p, x + 1)
                    axial = 0.5 * (high - low)
                    edge = pltpu.roll(edges, lanes - 2 * (e * cells_ax + x) - 2, 1)
                    inward = jnp.where(lane == 0, edge, pltpu.roll(centre, 1, 1))
                    outward = jnp.where(lane == lanes - 1, edge, pltpu.roll(centre, lanes - 1, 1))
                    radial = has_outer * outward - has_inner * inward
                    turned = (rate if p == 0 else -rate) * at(e, 1 - p, x)
                    for f in range(fields):
                        term = (
                            jac_axial[e, f] * axial
                            + jac_radial[e, f] * radial
                            + jac_swirl[e, f] * turned
                        )
                        if f == e:
                            term = term + centre
                        total[f] = term if e == 0 else total[f] + term
                for f in range(fields):
                    out[f, here, :] = total[f]
        return carry

    lax.fori_loop(0, half // chunk, step, 0)


def whole(shape):
    return pl.BlockSpec(shape, lambda i, where: (0,) * len(shape))


def stepped(shape):
    return pl.BlockSpec((1, *shape[1:]), lambda i, where: (i,) + (0,) * (len(shape) - 1))


def chosen(shape):
    return pl.BlockSpec((1, *shape[1:]), lambda i, where: (where[0],) + (0,) * (len(shape) - 1))


SMEM = pl.BlockSpec(memory_space=pltpu.SMEM)
ANY = pl.BlockSpec(memory_space=pl.ANY)


def call(kernel, steps, where, args, in_specs, outs, out_specs, scratch, flops):
    moved = sum(a.size * a.dtype.itemsize for a in args) + sum(o.size * o.dtype.itemsize for o in outs)
    return pl.pallas_call(
        kernel,
        grid_spec=pltpu.PrefetchScalarGridSpec(
            num_scalar_prefetch=1,
            grid=(steps,),
            in_specs=in_specs,
            out_specs=out_specs,
            scratch_shapes=scratch,
        ),
        out_shape=outs,
        compiler_params=pltpu.CompilerParams(vmem_limit_bytes=VMEM_LIMIT),
        cost_estimate=pl.CostEstimate(flops=flops, bytes_accessed=moved, transcendentals=0),
    )(where, *args)


def body(adjoint, state, wake, jac_axial, jac_radial, jac_swirl, wake_coupling):
    fields, modes, cells_ax, lanes = adjoint.shape
    groups = lax.axis_size("mode")
    count = groups * modes
    rad_size = lax.axis_size("rad")
    ax_size = lax.axis_size("ax")
    width = 2 if cells_ax % 2 == 0 else 1
    steps = cells_ax // width
    rows = modes * cells_ax
    cols = width * fields * lanes
    f32 = jnp.float32

    def cols_of(j, f):
        return pl.ds((j * fields + f) * lanes, lanes)

    dims = (fields, modes, cells_ax, width, cols_of)
    own_table, other_table, back_table = tables(groups, modes)
    where = jnp.stack([lax.axis_index("mode"), lax.axis_index("rad")]).astype(jnp.int32)

    adj = adjoint.reshape(fields, rows, lanes)
    st = state.reshape(fields, rows, lanes)
    wk = wake.reshape(rows, lanes)

    def fetch(value, s):
        return lax.ppermute(value, "mode", [((i + s) % groups, i) for i in range(groups)])

    def deliver(value, s):
        return lax.ppermute(value, "mode", [(i, (i + s) % groups) for i in range(groups)])

    adj_recv = [fetch(adj, s) for s in range(1, groups)]

    up = [(i, (i + 1) % ax_size) for i in range(ax_size)]
    down = [(i, (i - 1) % ax_size) for i in range(ax_size)]
    layer = jax.ShapeDtypeStruct((fields, modes, lanes), adjoint.dtype)
    first, last, edges = pl.pallas_call(
        functools.partial(pack_kernel, fields, modes, cells_ax),
        out_shape=[layer, layer, jax.ShapeDtypeStruct((modes, lanes), adjoint.dtype)],
        compiler_params=pltpu.CompilerParams(vmem_limit_bytes=VMEM_LIMIT),
    )(adj)
    below = lax.ppermute(last, "ax", up)
    above = lax.ppermute(first, "ax", down)
    below = jnp.where(lax.axis_index("ax") == 0, 0.0, below)
    above = jnp.where(lax.axis_index("ax") == ax_size - 1, 0.0, above)
    if rad_size == 2:
        inner = outer = lax.ppermute(edges, "rad", [(0, 1), (1, 0)])
    else:
        inner = lax.ppermute(edges, "rad", [(i, i + 1) for i in range(rad_size - 1)])
        outer = lax.ppermute(edges, "rad", [(i + 1, i) for i in range(rad_size - 1)])
    wake_recv = [fetch(wk, s) for s in range(1, groups)]

    field_shape = (fields, rows, lanes)
    angle_shape = (steps, count, cols)
    angle = jax.ShapeDtypeStruct(angle_shape, f32)
    field = jax.ShapeDtypeStruct(field_shape, f32)
    plane = jax.ShapeDtypeStruct((rows, lanes), f32)
    own_flops = 2 * 2 * 3 * count * modes * steps * cols

    a_own, c_own = call(
        functools.partial(own_kernel, dims), steps, where,
        (adj, st, wake_coupling, own_table),
        [whole(field_shape), whole(field_shape), SMEM, chosen(own_table.shape)],
        [angle, angle],
        [stepped(angle_shape), stepped(angle_shape)],
        [pltpu.VMEM((3 * modes, cols), jnp.bfloat16)] * 2,
        own_flops,
    )

    chunk = 16 if modes % 32 == 0 else 8
    base = call(
        functools.partial(
            base_kernel, fields, modes, cells_ax, chunk, count, lanes * rad_size, rad_size
        ),
        1, where,
        (adj, below, above, inner, outer, jac_axial, jac_radial, jac_swirl),
        [whole(field_shape), whole(below.shape), whole(above.shape)]
        + [whole(edges.shape)] * 2 + [SMEM] * 3,
        [field], [whole(field_shape)], [],
        32 * fields * fields * rows * lanes,
    )[0]

    cuts = (0, modes * 11 // 16 // 8 * 8, modes)
    pieces = len(cuts) - 1
    piece_rows = [(cuts[k + 1] - cuts[k]) * cells_ax for k in range(pieces)]
    joined = call(
        functools.partial(join_kernel, dims, groups, cuts), steps, where,
        (*adj_recv, a_own, c_own, other_table, base),
        [whole(field_shape)] * (groups - 1)
        + [stepped(angle_shape), stepped(angle_shape), chosen(other_table.shape), ANY],
        [angle] + [jax.ShapeDtypeStruct((n, lanes), f32) for n in piece_rows] * groups,
        [stepped(angle_shape)] + [whole((n, lanes)) for n in piece_rows] * groups,
        [pltpu.VMEM((3 * modes, cols), jnp.bfloat16)],
        (groups - 1) * own_flops // 2,
    )
    a_all = joined[0]
    parts = [joined[1 + k :: pieces] for k in range(pieces)]
    arrived = [[deliver(part[s], s) for s in range(1, groups)] for part in parts[:1]]
    if groups == 2 and rad_size == 2:
        sibling = lax.ppermute(parts[1][1], "rad", [(0, 1), (1, 0)])
        arrived.append([lax.ppermute(sibling, ("mode", "rad"), [(i, 3 - i) for i in range(4)])])
    else:
        arrived.append([deliver(parts[1][s], s) for s in range(1, groups)])

    adjoint_in = call(
        functools.partial(back_kernel, dims, groups), steps, where,
        (wk, *wake_recv, a_all, base, wake_coupling, back_table),
        [whole((rows, lanes))] * groups
        + [stepped(angle_shape), whole(field_shape), SMEM, chosen(back_table.shape)],
        [field], [whole(field_shape)],
        [pltpu.VMEM((2 * count, cols), jnp.bfloat16)],
        own_flops // 2,
    )[0]

    early, late = (functools.reduce(jnp.add, arrived[k], parts[k][0]) for k in range(pieces))
    wake_grad = -jnp.concatenate([early, late], axis=0)
    return (
        adjoint_in.reshape(adjoint.shape),
        wake_grad.reshape(wake.shape),
    )


def solution(mesh):
    return jax.shard_map(
        body,
        mesh=mesh,
        in_specs=(
            P(None, "mode", "ax", "rad"),
            P(None, "mode", "ax", "rad"),
            P("mode", "ax", "rad"),
            P(),
            P(),
            P(),
            P(),
        ),
        out_specs=(P(None, "mode", "ax", "rad"), P("mode", "ax", "rad")),
        check_vma=False,
    )
```
